256 devices in a mesh: req: 8 (over z_hi, y), tile: 32 (over x, z_lo, core).
Axes of the slice: x: 4, y: 4, z: 8 (z_hi: 2, z_lo: 4; z = z_hi * 4 + z_lo), core: 2. Of those that a mesh axis runs over, the one named last changes fastest.
Arguments:
- generator_latents: bfloat16 [8, 64, 32, 8, 512], P(None, 'req', 'tile'), may hold values from -40 to 40
- column_holder_map: int32 [8, 128, 1], P('req'), may hold values from 0 to 31; in each aligned block of 128 rows (0 to 127, 128 to 255, ..., all dimensions but the last counted through in order) at most 8 rows name the same one
- prior_frame_index: int32 [8], P('req'), may hold values from 0 to 3, as said below
- caches: bfloat16 [8, 2, 2, 64, 128, 512], P('req', None, None, 'tile'), may hold values from -6 to 6
- kernel_weight_pair: bfloat16 [2, 27, 512, 512], P(None, None, 'tile'), may hold values from -0.0546875 to 0.0546875
- group_norm_gain: float32 [2, 512], replicated, may hold values from 0.25 to 1.75
- group_norm_shift: float32 [2, 512], replicated, may hold values from -3 to 3
Outputs:
- upsampled: bfloat16 [8, 128, 256, 512], P('req', 'tile')
- new_inputs: bfloat16 [8, 2, 64, 128, 512], P('req', None, 'tile')
The draws below stay inside these ranges and needn't reach their ends.
Inputs may be any that keep to these rules, and one draw needn't show every extreme that they name: `column_holder_map`: for each request, each of the 32 holders owns at most 8 of the 128 columns; in some requests some holder owns exactly 8. `prior_frame_index`: some request has 3 and some other request has 0.
All inputs are finite; a program needn't handle non-finite values.
Results may differ from the reference program's by a relative error of at most 0.0095.
Values may be sent and summed in bfloat16 or wider, within the bound.
No kernel may reach another device: no remote copies, remote signals or barrier semaphores. Data moves between devices by JAX's collectives and lax.ppermute only.
A program may use at most 128 MiB of HBM per device.

```python
import math
import jax
import jax.numpy as jnp
import numpy as np
from jax import lax

BLOCK_CHANNELS = 512
GROUPS = 32
W = 128
LATENT_HEIGHT = 64
HOLDER_COLUMNS = 8
N_REQ = 8
N_TILE = 32


def field_scale(key, row_range):
    keys = jax.random.split(key, 2)
    rows = jnp.arange(LATENT_HEIGHT, dtype=jnp.float32) / max(LATENT_HEIGHT - 1, 1)
    row_scale = jnp.exp(row_range * (rows - 0.5))[None, :, None, None, None]
    column_scale = jnp.exp(jax.random.uniform(keys[0], (N_REQ, 1, N_TILE, HOLDER_COLUMNS, 1), jnp.float32, -1.15, 1.15))
    channel_scale = jnp.exp(jax.random.uniform(keys[1], (N_REQ, 1, 1, 1, BLOCK_CHANNELS), jnp.float32, -0.35, 0.35))
    return row_scale * column_scale * channel_scale


def draw_generator_latents(key, part):
    key = jax.random.fold_in(key, 11)
    keys = jax.random.split(key, 3)
    shape = (N_REQ, LATENT_HEIGHT, N_TILE, HOLDER_COLUMNS, BLOCK_CHANNELS)
    scale = field_scale(keys[0], 2.3)
    values = jnp.clip(jax.random.normal(keys[2], shape, jnp.float32), -3.0, 3.0) * scale
    return jnp.clip(values, -40.0, 40.0).astype(jnp.bfloat16)


def draw_prior_frame_index(key, part):
    key = jax.random.fold_in(key, 23)
    keys = jax.random.split(key, 2)
    order = jax.random.permutation(keys[0], N_REQ)
    values = jax.random.randint(keys[1], (N_REQ,), 0, 4, dtype=jnp.int32)
    values = values.at[order[0]].set(3)
    values = values.at[order[1]].set(0)
    return values.astype(jnp.int32)


def level_of(own_key, shape, pieces, smallest, high):
    def one(axis_at, parts):
        draws = jax.random.uniform(jax.random.fold_in(jax.random.fold_in(own_key, 6), axis_at), (parts,), jnp.float32, smallest / len(pieces), high / len(pieces))
        return jnp.repeat(jnp.exp(draws), shape[axis_at] // parts).reshape((-1,) + (1,) * (len(shape) - axis_at - 1))

    factor_of = one(*pieces[0])
    for cut in pieces[1:]:
        factor_of = factor_of * one(*cut)
    return factor_of


def deal_out(rng, own, number, rows, amount, top, most, lean):
    order = jax.random.permutation(rng, amount)
    crowded, usual = portions_of(amount, rows * top, most, lean, True), portions_of(amount, rows * top, most, lean, False)
    places = jnp.arange(amount)

    def named(lengths, turn):
        used = int((lengths > 0).sum())
        fixed = max(1, used // 4)
        moved = fixed + (places - fixed + turn * (used - fixed)) % max(1, amount - fixed)
        return jnp.zeros((amount,), jnp.int32).at[order[jnp.where(places < fixed, places, moved)]].set(jnp.asarray(lengths, jnp.int32))

    lengths = jnp.where(number % 4 == 0, named(crowded, number // 4), named(usual, number - number // 4 - 1))
    mixed = jax.random.permutation(jax.random.fold_in(own, 3), amount)
    source_of, sink = mixed[0:amount // 2 * 2:2], mixed[1:amount // 2 * 2:2]
    margin = jnp.minimum(lengths[source_of] - 1, most - lengths[sink]) // 2
    margin = jnp.where((source_of == order[0]) | (sink == order[0]) | (lengths[sink] == 0), 0, jnp.maximum(margin, 0))
    moved = jax.random.randint(jax.random.fold_in(own, 4), (amount // 2,), 0, 1 << 20) % (margin + 1)
    lengths = lengths.at[source_of].add(-moved).at[sink].add(moved)
    labels = jnp.searchsorted(jnp.cumsum(lengths), jnp.arange(rows * top), side="right").astype(jnp.int32)
    grid = labels.reshape(top, rows).T
    grid = grid[jax.random.permutation(jax.random.fold_in(own, 1), rows)]
    turn = jax.random.randint(jax.random.fold_in(own, 2), (rows, 1), 0, top)
    return jnp.take_along_axis(grid, (jnp.arange(top)[None, :] + turn) % top, axis=1)


def portions_of(number_of, total, bound, slope, full):
    weights = [(1 << 20) // math.isqrt(standing ** slope) + 1 for standing in range(1, number_of + 1)]
    largest = bound if full else min(bound, max(-(-total // number_of), total * weights[0] // sum(weights)))
    least = 1 if total - largest >= number_of - 1 else 0
    given, rest = [largest] + [least] * (number_of - 1), total - largest - least * (number_of - 1)
    while rest > 0:
        movable = [i for i in range(1, number_of) if given[i] < largest] or [i for i in range(1, number_of) if given[i] < bound]
        whole, budget = sum([weights[i] for i in movable]), rest
        for i in movable:
            more = min(bound - given[i], max(1, budget * weights[i] // whole), rest)
            given[i] = given[i] + more
            rest = rest - more
    return np.array(given)


def scatter_about(key, extent, scale, most, cuts=(), kind=jnp.bfloat16):
    values = scale * jax.random.normal(key, extent, jnp.float32)
    if cuts:
        values = values * level_of(key, extent, cuts, -0.22, 0.18)
    return jnp.clip(values, -most, most).astype(kind)


def setup_inputs(seed: int = 0) -> dict:
    splits = jax.random.split(jax.random.key(seed), 8)
    generator_latents = draw_generator_latents(jax.random.fold_in(splits[7], 71), 0)
    column_holder_map_keys = jax.random.split(jax.random.fold_in(splits[1], 1), N_REQ * W // W)
    column_holder_map_turns = jax.random.permutation(jax.random.fold_in(splits[1], 3), N_REQ * W // W)
    column_holder_map = jax.vmap(lambda own, number: deal_out(jax.random.fold_in(splits[1], 2), own, number, W, N_TILE, 1, HOLDER_COLUMNS, 2))(column_holder_map_keys, column_holder_map_turns).reshape((N_REQ, W, 1))
    prior_frame_index = draw_prior_frame_index(jax.random.fold_in(splits[7], 71), 0)
    caches = scatter_about(splits[3], (N_REQ, 2, 2, LATENT_HEIGHT, W, BLOCK_CHANNELS), 1.0, 6.0, ((0, 8), (3, 32)))
    kernel_weight_pair = scatter_about(splits[4], (2, 27, BLOCK_CHANNELS, BLOCK_CHANNELS), (27 * BLOCK_CHANNELS) ** -0.5, 0.0546875, ((2, 32),))
    group_norm_gain = jnp.clip(1.0 + 0.15 * jax.random.normal(splits[5], (2, BLOCK_CHANNELS), jnp.float32), 0.25, 1.75)
    group_norm_shift = scatter_about(splits[6], (2, BLOCK_CHANNELS), 0.5, 3.0, (), jnp.float32)
    return {"generator_latents": generator_latents, "column_holder_map": column_holder_map, "prior_frame_index": prior_frame_index, "caches": caches, "kernel_weight_pair": kernel_weight_pair, "group_norm_gain": group_norm_gain, "group_norm_shift": group_norm_shift}


EPS = 1e-06

def column_index(owner, holders, most):
    hits = (owner[:, None] == jnp.arange(holders, dtype=jnp.int32)[None, :]).astype(jnp.int32)
    before = jnp.cumsum(hits, axis=0) - hits
    slot = lax.optimization_barrier(jnp.sum(before * hits, axis=1)).astype(jnp.int32)
    return (owner * most + slot).astype(jnp.int32)

def group_norm(values, gain, shift, groups):
    height, width, channels = values.shape
    grouped = values.reshape(height, width, groups, channels // groups)
    mean = lax.optimization_barrier(jnp.mean(grouped, axis=(0, 1, 3), keepdims=True))
    spread = lax.optimization_barrier(jnp.mean(jnp.square(grouped - mean), axis=(0, 1, 3), keepdims=True))
    normed = ((grouped - mean) * lax.rsqrt(spread + EPS)).reshape(height, width, channels)
    return normed * gain + shift

def with_history(history, current, position):
    newer = jnp.where(position >= 1, history[1], current)
    older = jnp.where(position >= 2, history[0], newer)
    return jnp.stack([older, newer, current])

def causal_conv(frames, kernel):
    depth, height, width, channels = frames.shape
    padded = jnp.pad(frames, ((0, 0), (1, 1), (1, 1), (0, 0)))
    total = jnp.zeros((height * width, kernel.shape[2]), jnp.float32)
    for tap in range(27):
        frame_tap, row_tap, col_tap = (tap // 9, tap // 3 % 3, tap % 3)
        window = padded[frame_tap, row_tap:row_tap + height, col_tap:col_tap + width, :].reshape(height * width, channels)
        total = total + jnp.dot(window, kernel[tap], preferred_element_type=jnp.float32)
    return total.reshape(height, width, kernel.shape[2])

def reference(generator_latents, column_holder_map, prior_frame_index, caches, kernel_weight_pair, group_norm_gain, group_norm_shift):
    outputs = []
    inputs = []
    for request_number in range(N_REQ):
        loop_index = column_index(column_holder_map[request_number, :, 0], N_TILE, HOLDER_COLUMNS)
        frame_number = jnp.take(generator_latents[request_number].reshape(LATENT_HEIGHT, N_TILE * HOLDER_COLUMNS, BLOCK_CHANNELS), loop_index, axis=1)
        position = prior_frame_index[request_number]
        first = jax.nn.silu(group_norm(frame_number.astype(jnp.float32), group_norm_gain[0], group_norm_shift[0], GROUPS)).astype(jnp.bfloat16)
        hidden = causal_conv(with_history(caches[request_number, 0], first, position), kernel_weight_pair[0]).astype(jnp.bfloat16)
        second = jax.nn.silu(group_norm(hidden.astype(jnp.float32), group_norm_gain[1], group_norm_shift[1], GROUPS)).astype(jnp.bfloat16)
        branch = causal_conv(with_history(caches[request_number, 1], second, position), kernel_weight_pair[1])
        joined = (frame_number.astype(jnp.float32) + branch).astype(jnp.bfloat16)
        outputs.append(jnp.repeat(jnp.repeat(joined, 2, axis=0), 2, axis=1))
        inputs.append(jnp.stack([first, second]))
    return (jnp.stack(outputs), jnp.stack(inputs))
```

```python
import functools

import jax
import jax.numpy as jnp
from jax import lax
from jax.experimental import pallas as pl
from jax.experimental.pallas import tpu as pltpu
from jax.sharding import PartitionSpec as P

GROUPS = 32
EPS = 1e-06
NX, NY, NZ = 4, 4, 8
CH = 512
HALF = CH // 2
TAPS = 27
WIDTH = 128
ROWS = 2
SHARD = CH // 32
BOTH = ("req", "tile")
BF, F32 = jnp.bfloat16, jnp.float32


def joint(x, y, z, core):
    return ((z // 4) * NY + y) * 32 + x * 8 + (z % 4) * 2 + core


def torus_perm(dx=0, dz=0, flip=0):
    perm = []
    for x in range(NX):
        for y in range(NY):
            for z in range(NZ):
                for core in range(2):
                    src = joint((x + dx) % NX, y, (z + dz) % NZ, core ^ flip)
                    perm.append((src, joint(x, y, z, core)))
    return perm


def from_torus(array, dx=0, dz=0):
    return lax.ppermute(array, BOTH, torus_perm(dx, dz))


def swap_cores(array):
    return lax.ppermute(array, "tile", [(i, i ^ 1) for i in range(32)])


def combine(parts, count):
    number = len(parts)
    mean = sum(p[0] for p in parts) / number
    spread = sum(p[1] for p in parts)
    spread = spread + count * sum(jnp.square(p[0] - mean) for p in parts)
    return jnp.stack([mean, spread])


def merge_stats(stats, count, steps):
    for stride, size in steps:
        received = [stats]
        for k in range(1, size):
            perm = []
            for i in range(32):
                digit = (i // stride) % size
                perm.append((i, i + (((digit + k) % size) - digit) * stride))
            received.append(lax.ppermute(stats, "tile", perm))
        stats = combine(received, count)
        count = count * size
    return stats, count


def group_matrix(channels):
    per = CH // GROUPS
    row = lax.broadcasted_iota(jnp.int32, (channels, channels), 0) // per
    col = lax.broadcasted_iota(jnp.int32, (channels, channels), 1) // per
    return jnp.where(row == col, 1.0, 0.0).astype(F32)


def local_stats(values):
    cells, channels = values.shape
    ones = group_matrix(channels)
    total = jnp.sum(values, axis=0, keepdims=True)
    dot = functools.partial(jnp.dot, preferred_element_type=F32, precision=lax.Precision.HIGHEST)
    mean = dot(jnp.broadcast_to(total, (8, channels)), ones)[:1] / (cells * (CH // GROUPS))
    off = values - mean
    spread = dot(jnp.broadcast_to(jnp.sum(off * off, axis=0, keepdims=True), (8, channels)), ones)[:1]
    return mean, spread


def frame_kernel(index_ref, placed_ref, frame_ref, stats_ref):
    index = index_ref[...]
    lane = lax.broadcasted_iota(jnp.int32, (WIDTH, CH), 1)
    placed = placed_ref[...].reshape(CH, CH)
    rows = []
    for row in range(ROWS):
        pick = jnp.where(lane == index + 8 * row, 1.0, 0.0).astype(BF)
        rows.append(jnp.dot(pick, placed, preferred_element_type=F32))
        frame_ref[row] = rows[row].astype(BF)
    mean, spread = local_stats(jnp.concatenate(rows, axis=0))
    stats_ref[0:1, :] = mean
    stats_ref[1:2, :] = spread


def pack_kernel(conv, m0, m1, m3, m2, g0, g1, g3, g2, m_out, g_out, sem):
    copies = []
    for k, (src, out) in enumerate(
        [(s, m_out) for s in (m0, m1, m3, m2)] + [(s, g_out) for s in (g0, g1, g3, g2)]
    ):
        src = src.at[conv] if len(src.shape) == 4 else src
        copies.append(pltpu.make_async_copy(src, out.at[k % 4], sem.at[k]))
        copies[-1].start()
    for copy in copies:
        copy.wait()


def pack(conv, arrays):
    shape = jax.ShapeDtypeStruct((4, TAPS, SHARD, HALF), BF)
    anyspec = pl.BlockSpec(memory_space=pl.ANY)
    return pl.pallas_call(
        functools.partial(pack_kernel, conv),
        out_shape=(shape, shape),
        in_specs=[anyspec] * 8,
        out_specs=(anyspec, anyspec),
        scratch_shapes=[pltpu.SemaphoreType.DMA((8,))],
        cost_estimate=pl.CostEstimate(flops=0, bytes_accessed=4 * 10**6, transcendentals=0),
        name="pack%d" % conv,
    )(*arrays)


def silu(v):
    return v / (1.0 + jnp.exp(-v))


def load_weights(place, blocks, weights, sems):
    x, z, core = place
    order = (0, 1, 3, 2)
    m_own, m_up, m_down, m_far_a, m_far_b, g_own, g_up, g_down, g_far_a, g_far_b = blocks
    pieces = []
    for kind, (own, up, down, far_a, far_b) in enumerate(
        ((m_own, m_up, m_down, m_far_a, m_far_b), (g_own, g_up, g_down, g_far_a, g_far_b))
    ):
        for along, ref in ((0, own), (1, up), (3, down)):
            for k in range(4):
                pieces.append((kind, along, order[k], ref, k))
        for k in range(2):
            pieces.append((kind, 2, order[k], far_a, k))
            pieces.append((kind, 2, order[2 + k], far_b, k))
    for a in range(3):
        for kind, along, across, ref, k in pieces:
            dx, dz = (across, along) if kind == 0 else (along, across)
            holder = lax.rem(x + dx, 4) * 8 + lax.rem(z + dz, 4) * 2
            holder = holder + (core if kind == 0 else 1 - core)
            row = pl.multiple_of(holder * SHARD, SHARD)
            pltpu.make_async_copy(
                ref.at[k, pl.ds(9 * a, 9)],
                weights.at[pl.ds(9 * a, 9), pl.ds(row, SHARD), :],
                sems.at[a],
            ).start()


def wait_weights(a, weights, sems):
    part = weights.at[pl.ds(9 * a, 9)]
    pltpu.make_async_copy(part, part, sems.at[a]).wait()


def convolve(frames, weights, sems, acc, older, newer):
    for a, which in ((0, older), (1, newer), (2, 2)):
        wait_weights(a, weights, sems)
        for b in range(3):
            slab = frames[which, pl.ds(b, 4)].reshape(4 * WIDTH, CH)
            for c in range(3):
                part = jnp.dot(slab, weights[9 * a + 3 * b + c], preferred_element_type=F32)
                if a == 0 and b == 0:
                    acc[c] = part
                else:
                    acc[c] += part
    column = lax.broadcasted_iota(jnp.int32, (4 * WIDTH, HALF), 0) % WIDTH
    left = jnp.where(column == 0, 0.0, pltpu.roll(acc[0], 1, 0))
    right = jnp.where(column == WIDTH - 1, 0.0, pltpu.roll(acc[2], 4 * WIDTH - 1, 0))
    return acc[1] + left + right


def cached_copies(conv, core, caches, halo, partner, frames, sems):
    own = 1 + 2 * core
    other = 3 - 2 * core
    own_edge = 5 * core
    other_edge = 5 - 5 * core
    result = []
    for src, start, size in (
        (caches.at[0, conv], own, 2),
        (halo.at[conv], own_edge, 1),
        (partner.at[conv, :, pl.ds(0, 2)], other, 2),
        (partner.at[conv, :, pl.ds(2, 1)], other_edge, 1),
    ):
        result.append(
            pltpu.make_async_copy(
                src, frames.at[pl.ds(0, 2), pl.ds(start, size)], sems.at[3 + len(result)]
            )
        )
    return result


def conv_one_kernel(
    info, scale, own, swapped, near, far, caches, halo, partner, *rest
):
    blocks, (hidden_ref, first_ref, stats_ref, frames, weights, acc, sems) = rest[:10], rest[10:]
    x, z, core, older, newer, top, bottom = (info[k] for k in range(7))
    load_weights((x, z, core), blocks, weights, sems)
    copies = cached_copies(0, core, caches, halo, partner, frames, sems)
    for copy in copies:
        copy.start()
    mean, gain, shift = scale[0:1, :], scale[1:2, :], scale[2:3, :]

    def norm(values):
        return silu((values.astype(F32) - mean) * gain + shift).astype(BF)

    for row in range(ROWS):
        mine = norm(own[row])
        first_ref[row] = mine
        frames[2, 1 + 2 * core + row] = mine
        frames[2, 3 - 2 * core + row] = norm(swapped[row])
    upper = jnp.where(core == 0, near[0], far[0])
    lower = jnp.where(core == 0, far[0], near[0])
    frames[2, 0] = jnp.where(top == 1, jnp.zeros((WIDTH, CH), BF), norm(upper))
    frames[2, 5] = jnp.where(bottom == 1, jnp.zeros((WIDTH, CH), BF), norm(lower))
    for copy in copies:
        copy.wait()
    total = convolve(frames, weights, sems, acc, older, newer).astype(BF)
    hidden_ref[...] = total.reshape(4, WIDTH, HALF)
    mean2, spread2 = local_stats(total.astype(F32))
    stats_ref[0:1, :] = mean2
    stats_ref[1:2, :] = spread2


def conv_two_kernel(
    info, scale, scale_other, own, up, down, other, frame, swapped, caches, halo, partner, *rest
):
    blocks, (mine_ref, theirs_ref, second_ref, frames, weights, acc, sems) = rest[:10], rest[10:]
    x, z, core, older, newer, top, bottom = (info[k] for k in range(7))
    load_weights((x, z, core), blocks, weights, sems)
    copies = cached_copies(1, core, caches, halo, partner, frames, sems)
    for copy in copies:
        copy.start()

    def norm(values, table):
        values = (values.astype(F32) - table[0:1, :]) * table[1:2, :] + table[2:3, :]
        return silu(values).astype(BF)

    mine = pl.ds(pl.multiple_of(core * HALF, HALF), HALF)
    theirs = pl.ds(pl.multiple_of((1 - core) * HALF, HALF), HALF)
    zeros = jnp.zeros((WIDTH, HALF), BF)
    for row in range(4):
        frames[2, 1 + row, :, mine] = norm(own[row], scale)
        frames[2, 1 + row, :, theirs] = norm(other[1 + row], scale_other)
    frames[2, 0, :, mine] = jnp.where(top == 1, zeros, norm(up[0], scale))
    frames[2, 0, :, theirs] = jnp.where(top == 1, zeros, norm(other[0], scale_other))
    frames[2, 5, :, mine] = jnp.where(bottom == 1, zeros, norm(down[0], scale))
    frames[2, 5, :, theirs] = jnp.where(bottom == 1, zeros, norm(other[5], scale_other))
    for row in range(ROWS):
        second_ref[row] = frames[2, 1 + 2 * core + row]
    for copy in copies:
        copy.wait()
    branch = convolve(frames, weights, sems, acc, older, newer).reshape(4, WIDTH, HALF)
    acc[0] = branch.reshape(4 * WIDTH, HALF)
    for row in range(ROWS):
        start = pl.multiple_of((2 * core + row) * WIDTH, WIDTH)
        joined = frame[row, :, mine].astype(F32) + acc[0, pl.ds(start, WIDTH), :]
        mine_ref[row] = joined.astype(BF)
        start = pl.multiple_of((2 - 2 * core + row) * WIDTH, WIDTH)
        joined = swapped[row, :, mine].astype(F32) + acc[0, pl.ds(start, WIDTH), :]
        theirs_ref[row] = joined.astype(BF)


def conv_call(kernel, name, out_shape, vmem_inputs, any_inputs, info):
    vmem = pl.BlockSpec(memory_space=pltpu.VMEM)
    anyspec = pl.BlockSpec(memory_space=pl.ANY)
    return pl.pallas_call(
        kernel,
        out_shape=out_shape,
        in_specs=[pl.BlockSpec(memory_space=pltpu.SMEM)]
        + [vmem] * len(vmem_inputs)
        + [anyspec] * len(any_inputs),
        out_specs=tuple(vmem for _ in out_shape),
        scratch_shapes=[
            pltpu.VMEM((3, 6, WIDTH, CH), BF),
            pltpu.VMEM((TAPS, CH, HALF), BF),
            pltpu.VMEM((3, 4 * WIDTH, HALF), F32),
            pltpu.SemaphoreType.DMA((7,)),
        ],
        compiler_params=pltpu.CompilerParams(vmem_limit_bytes=40 * 2**20),
        cost_estimate=pl.CostEstimate(
            flops=2 * 512 * TAPS * CH * HALF, bytes_accessed=12 * 10**6, transcendentals=400000
        ),
        name=name,
    )(info, *vmem_inputs, *any_inputs)


def scale_table(stats, count, gain, shift):
    mean, spread = stats[0], stats[1] / count
    return jnp.stack([mean, lax.rsqrt(spread + EPS) * gain, shift])


def per_device(
    generator_latents,
    column_holder_map,
    prior_frame_index,
    caches,
    kernel_weight_pair,
    group_norm_gain,
    group_norm_shift,
):
    tile = lax.axis_index("tile")
    core = tile % 2
    position = prior_frame_index[0]
    older = jnp.where(position >= 2, 0, jnp.where(position == 1, 1, 2))
    newer = jnp.where(position >= 1, 1, 2)
    info = jnp.stack(
        [tile // 8, tile // 2 % 4, core, older, newer, tile // 2 == 0, tile // 2 == 15]
    ).astype(jnp.int32)

    placed = lax.all_to_all(generator_latents, "req", split_axis=0, concat_axis=0, tiled=True)

    mine = lax.dynamic_slice_in_dim(kernel_weight_pair, core * HALF, HALF, axis=3)
    theirs = lax.dynamic_slice_in_dim(kernel_weight_pair, (1 - core) * HALF, HALF, axis=3)
    got = swap_cores(theirs)
    m1, m3 = from_torus(mine, dx=1), from_torus(mine, dx=-1)
    g1, g3 = from_torus(got, dz=1), from_torus(got, dz=-1)
    m2 = [from_torus(mine[0], dx=2), from_torus(mine[1], dx=-2)]
    g2 = [from_torus(got[0], dz=2), from_torus(got[1], dz=-2)]
    blocks = []
    for conv in range(2):
        m_own, g_own = pack(conv, (mine, m1, m3, m2[conv], got, g1, g3, g2[conv]))
        m_up, m_down = from_torus(m_own, dz=1), from_torus(m_own, dz=-1)
        g_up, g_down = from_torus(g_own, dx=1), from_torus(g_own, dx=-1)
        m_far_a, m_far_b = from_torus(m_up[:2], dz=1), from_torus(m_down[2:], dz=-1)
        g_far_a, g_far_b = from_torus(g_up[:2], dx=1), from_torus(g_down[2:], dx=-1)
        blocks.append(
            [m_own, m_up, m_down, m_far_a, m_far_b, g_own, g_up, g_down, g_far_a, g_far_b]
        )

    to_next = [(i, i + 1 if i % 2 else i - 1) for i in range(1, 31)]
    to_far = [(i, i + 2 if i % 2 else i - 2) for i in range(32) if 0 <= (i + 2 if i % 2 else i - 2) < 32]
    edge = lax.dynamic_slice_in_dim(caches[0], core, 1, axis=2)
    halo = lax.ppermute(edge, "tile", to_next)
    partner = swap_cores(jnp.concatenate([caches[0], halo], axis=2))

    owner = column_holder_map[0, :, 0]
    hits = (owner[:, None] == jnp.arange(32, dtype=jnp.int32)[None, :]).astype(jnp.int32)
    slot = jnp.sum((jnp.cumsum(hits, axis=0) - hits) * hits, axis=1)
    index = (owner * 16 + slot).astype(jnp.int32)[:, None]

    placed = lax.all_to_all(
        placed.reshape(32, 16, CH), "tile", split_axis=0, concat_axis=0, tiled=True
    )
    frame, stats = pl.pallas_call(
        frame_kernel,
        out_shape=(
            jax.ShapeDtypeStruct((ROWS, WIDTH, CH), BF),
            jax.ShapeDtypeStruct((2, CH), F32),
        ),
        compiler_params=pltpu.CompilerParams(vmem_limit_bytes=16 * 2**20),
        cost_estimate=pl.CostEstimate(flops=3 * 10**8, bytes_accessed=10**6, transcendentals=0),
        name="frame",
    )(index, placed)

    edge = lax.dynamic_slice_in_dim(frame, core, 1, axis=0)
    near, far = lax.ppermute(edge, "tile", to_next), lax.ppermute(edge, "tile", to_far)
    swapped = swap_cores(frame)
    per = CH // GROUPS
    stats, count = merge_stats(stats, ROWS * WIDTH * per, ((1, 2), (2, 4), (8, 4)))
    table = scale_table(stats, count, group_norm_gain[0], group_norm_shift[0])
    hidden, first, stats = conv_call(
        conv_one_kernel,
        "conv_one",
        (
            jax.ShapeDtypeStruct((4, WIDTH, HALF), BF),
            jax.ShapeDtypeStruct((ROWS, WIDTH, CH), BF),
            jax.ShapeDtypeStruct((2, HALF), F32),
        ),
        (table, frame, swapped, near, far),
        (caches, halo, partner, *blocks[0]),
        info,
    )

    up = lax.ppermute(hidden[3:4], "tile", [(i, i + 2) for i in range(30)])
    down = lax.ppermute(hidden[0:1], "tile", [(i + 2, i) for i in range(30)])
    other = swap_cores(jnp.concatenate([up, hidden, down], axis=0))
    stats, count = merge_stats(stats, 4 * WIDTH * per, ((2, 4), (8, 4)))
    stats_other = swap_cores(stats)
    cut = lambda array, start: lax.dynamic_slice_in_dim(array, start * HALF, HALF, axis=0)
    gain, shift = group_norm_gain[1], group_norm_shift[1]
    table = scale_table(stats, count, cut(gain, core), cut(shift, core))
    table_other = scale_table(stats_other, count, cut(gain, 1 - core), cut(shift, 1 - core))
    half = jax.ShapeDtypeStruct((ROWS, WIDTH, HALF), BF)
    joined, theirs, second = conv_call(
        conv_two_kernel,
        "conv_two",
        (half, half, jax.ShapeDtypeStruct((ROWS, WIDTH, CH), BF)),
        (table, table_other, hidden, up, down, other, frame, swapped),
        (caches, halo, partner, *blocks[1]),
        info,
    )
    received = swap_cores(theirs)
    joined = jnp.where(
        core == 0,
        jnp.concatenate([joined, received], axis=2),
        jnp.concatenate([received, joined], axis=2),
    )
    upsampled = jnp.repeat(jnp.repeat(joined, 2, axis=0), 2, axis=1)
    return (upsampled[None], jnp.stack([first, second])[None])


def solution(mesh):
    in_specs = (
        P(None, "req", "tile", None, None),
        P("req", None, None),
        P("req"),
        P("req", None, None, "tile", None, None),
        P(None, None, "tile", None),
        P(),
        P(),
    )
    out_specs = (P("req", "tile", None, None), P("req", None, "tile", None, None))
    return jax.shard_map(
        per_device, mesh=mesh, in_specs=in_specs, out_specs=out_specs, check_vma=False
    )
```

```python
import functools

import jax
import jax.numpy as jnp
import numpy as np
from jax import lax
from jax.experimental import pallas as pl
from jax.experimental.pallas import tpu as pltpu
from jax.sharding import PartitionSpec as P

GROUPS = 32
EPS = 1e-06
CH = 512
TEAM = 2
PART = CH // TEAM
PER = CH // GROUPS
WIDTH = 128
ROWS = 2
CELLS = ROWS * WIDTH
TILES = 32
BF, F32 = jnp.bfloat16, jnp.float32


def from_team(array, j):
    return lax.ppermute(array, "req", [(i, i ^ j) for i in range(8)])


def from_above(array):
    return lax.ppermute(array, "tile", [(i, i + 1) for i in range(TILES - 1)])


def from_below(array):
    return lax.ppermute(array, "tile", [(i + 1, i) for i in range(TILES - 1)])


dot32 = functools.partial(jnp.dot, preferred_element_type=F32, precision=lax.Precision.HIGHEST)


def spread_lanes(channels, first_lane, transposed=False):
    shape = (128, channels) if transposed else (channels, 128)
    lane = lax.broadcasted_iota(jnp.int32, shape, 0 if transposed else 1)
    channel = lax.broadcasted_iota(jnp.int32, shape, 1 if transposed else 0)
    return jnp.where(lane == first_lane + channel // PER, 1.0, 0.0).astype(F32)


def local_stats(values):
    cells, channels = values.shape
    total = jnp.sum(values, axis=0, keepdims=True) / (cells * PER)
    mean = dot32(jnp.broadcast_to(total, (8, channels)), spread_lanes(channels, 0))
    off = values - dot32(mean, spread_lanes(channels, 0, True))[:1]
    square = jnp.broadcast_to(jnp.sum(off * off, axis=0, keepdims=True), (8, channels))
    return mean + dot32(square, spread_lanes(channels, GROUPS))


def join_stats(stats):
    lane = lax.broadcasted_iota(jnp.int32, (TILES, 128), 1)
    mean = jnp.sum(jnp.where(lane < GROUPS, stats, 0.0), axis=0, keepdims=True) / TILES
    off = jnp.where(lane < GROUPS, stats - mean, 0.0)
    between = jnp.sum(off * off, axis=0, keepdims=True) / TILES
    within = jnp.where(lane >= GROUPS, stats, 0.0)
    within = jnp.sum(within, axis=0, keepdims=True) / (TILES * CELLS * PER)
    return tuple(jnp.broadcast_to(v, (8, 128)) for v in (mean, within, between))


def norm_table(joined):
    mean, within, between = joined
    back = spread_lanes(CH, 0, True)
    spread = dot32(within, spread_lanes(CH, GROUPS, True)) + dot32(between, back)
    return dot32(mean, back)[:1], lax.rsqrt(spread[:1] + EPS)


def flagged(stats, flag):
    lane = lax.broadcasted_iota(jnp.int32, (TILES, 128), 1)
    return jnp.where(lane == 64, flag.astype(F32), jnp.broadcast_to(stats[:1], (TILES, 128)))


def flag_of(stats):
    lane = lax.broadcasted_iota(jnp.int32, (8, 128), 1)
    return jnp.max(jnp.where(lane == 64, stats[0:8, :], 0.0)) > 0.5


def silu(v):
    return v / (1.0 + jnp.exp(-v))


def norm(values, table):
    return silu((values.astype(F32) - table[0]) * table[1] + table[2]).astype(BF)


def frame_kernel(info, index_ref, placed_ref, frame_ref, stats_ref):
    index = index_ref[...]
    lane = lax.broadcasted_iota(jnp.int32, (WIDTH, CH), 1)
    placed = placed_ref[...].reshape(CH, CH)
    rows = []
    for row in range(ROWS):
        pick = jnp.where(lane == index + 8 * row, 1.0, 0.0).astype(BF)
        rows.append(jnp.dot(pick, placed, preferred_element_type=F32))
        frame_ref[row] = rows[row].astype(BF)
    stats_ref[...] = flagged(local_stats(jnp.concatenate(rows, axis=0)), info[3])


VMEM = pl.BlockSpec(memory_space=pltpu.VMEM)
SMEM = pl.BlockSpec(memory_space=pltpu.SMEM)
ANY = pl.BlockSpec(memory_space=pl.ANY)


def shape(*sizes):
    return jax.ShapeDtypeStruct(sizes, BF)


def edges_kernel(*refs):
    sources, (last, first) = refs[:TEAM], refs[TEAM:]
    for j, source in enumerate(sources):
        for lead in np.ndindex(source.shape[:-3]):
            last[(j, *lead)] = source[(*lead, ROWS - 1)]
            first[(j, *lead)] = source[(*lead, 0)]


def edges(slots):
    sizes = slots[0].shape
    out = shape(TEAM, *sizes[:-3], *sizes[-2:])
    last, first = pl.pallas_call(
        edges_kernel,
        out_shape=(out, out),
        in_specs=[VMEM] * TEAM,
        out_specs=(VMEM, VMEM),
        compiler_params=pltpu.CompilerParams(vmem_limit_bytes=12 * 2**20),
        cost_estimate=pl.CostEstimate(flops=0, bytes_accessed=10**6, transcendentals=0),
        name="edges",
    )(*slots)
    return from_above(last), from_below(first)


def start_loads(conv, kernels, earlier, above, below, weights, frames, sems):
    for a in range(3):
        part = pl.ds(9 * a, 9)
        pltpu.make_async_copy(kernels.at[conv, part], weights.at[part], sems.at[a]).start()
    copies = []
    for j in range(TEAM):
        for a in range(2):
            for src, dst in (
                (earlier[j].at[conv, a], frames.at[a, j, pl.ds(1, ROWS)]),
                (above.at[j, conv, a], frames.at[a, j, 0]),
                (below.at[j, conv, a], frames.at[a, j, ROWS + 1]),
            ):
                copies.append(pltpu.make_async_copy(src, dst, sems.at[3 + len(copies)]))
                copies[-1].start()
    return copies


def finish_history(parts, copies, frames):
    for copy in copies:
        copy.wait()
    for j, part in enumerate(parts):

        @pl.when(flag_of(part))
        def _():
            for row in range(ROWS + 2):
                frames[0, j, row] = frames[2, j, row]
                frames[1, j, row] = frames[2, j, row]


def convolve(frames, weights, sems, acc):
    cells = TEAM * CELLS
    for a in range(3):
        part = weights.at[pl.ds(9 * a, 9)]
        pltpu.make_async_copy(part, part, sems.at[a]).wait()
        for b in range(3):
            slab = frames[a, :, pl.ds(b, ROWS)].reshape(cells, CH)
            for c in range(3):
                tap = weights[9 * a + 3 * b + c]
                product = jnp.dot(slab, tap, preferred_element_type=F32)
                if a == 0 and b == 0:
                    acc[c] = product
                else:
                    acc[c] += product
    column = lax.broadcasted_iota(jnp.int32, (cells, PART), 0) % WIDTH
    left = jnp.where(column == 0, 0.0, pltpu.roll(acc[0], 1, 0))
    right = jnp.where(column == WIDTH - 1, 0.0, pltpu.roll(acc[2], cells - 1, 0))
    return acc[1] + left + right


def unpack(stats, rest):
    others = TEAM - 1
    team, (above, below) = rest[:others], rest[others : others + 2]
    end = others + 2 + others
    return team, above, below, (stats,) + rest[others + 2 : end], rest[end:]


def conv_one_kernel(info, stats, gain, shift, own, *rest):
    team, above, below, parts, rest = unpack(stats, rest)
    earlier, (old_above, old_below, kernels), rest = rest[:TEAM], rest[TEAM : TEAM + 3], rest[TEAM + 3 :]
    hidden_ref, first_ref, stats_ref, frames, weights, acc, sems = rest
    copies = start_loads(0, kernels, earlier, old_above, old_below, weights, frames, sems)
    zeros = jnp.zeros((WIDTH, CH), BF)
    for j, (frame, part) in enumerate(zip((own,) + team, parts)):
        mean, scale = norm_table(join_stats(part[...]))
        table = (mean, scale * gain[0:1, :], shift[0:1, :])
        for row in range(ROWS):
            frames[2, j, 1 + row] = norm(frame[row], table)
        frames[2, j, 0] = jnp.where(info[1] == 1, zeros, norm(above[j], table))
        frames[2, j, ROWS + 1] = jnp.where(info[2] == 1, zeros, norm(below[j], table))
    for row in range(ROWS):
        first_ref[row] = frames[2, 0, 1 + row]
    finish_history(parts, copies, frames)
    total = convolve(frames, weights, sems, acc).astype(BF)
    hidden_ref[...] = total.reshape(TEAM, ROWS, WIDTH, PART)
    total = total.astype(F32)
    total = jnp.concatenate([total[j * CELLS : (j + 1) * CELLS] for j in range(TEAM)], axis=1)
    stats_ref[...] = flagged(local_stats(total), info[3])


def conv_two_kernel(info, stats, gain, shift, own, *rest):
    team, above, below, parts, rest = unpack(stats, rest)
    raw, rest = rest[:TEAM], rest[TEAM:]
    earlier, (old_above, old_below, kernels), rest = rest[:TEAM], rest[TEAM : TEAM + 3], rest[TEAM + 3 :]
    joined_refs, (second_ref, frames, weights, acc, sems) = rest[:TEAM], rest[TEAM:]
    copies = start_loads(1, kernels, earlier, old_above, old_below, weights, frames, sems)
    zeros = jnp.zeros((WIDTH, PART), BF)
    for k, (hidden, part) in enumerate(zip((own,) + team, parts)):
        mean, scale = norm_table(join_stats(part[...]))
        lanes = pl.ds(pl.multiple_of((info[0] ^ k) * PART, PART), PART)
        gains, shifts = gain[1:2, lanes], shift[1:2, lanes]
        for j in range(TEAM):
            here = slice((j ^ k) * PART, (j ^ k) * PART + PART)
            table = (mean[:, here], scale[:, here] * gains, shifts)
            for row in range(ROWS):
                frames[2, j, 1 + row, :, lanes] = norm(hidden[j ^ k, row], table)
            frames[2, j, 0, :, lanes] = jnp.where(info[1] == 1, zeros, norm(above[k, j ^ k], table))
            frames[2, j, ROWS + 1, :, lanes] = jnp.where(
                info[2] == 1, zeros, norm(below[k, j ^ k], table)
            )
    for row in range(ROWS):
        second_ref[row] = frames[2, 0, 1 + row]
    finish_history(parts, copies, frames)
    branch = convolve(frames, weights, sems, acc).reshape(TEAM, ROWS, WIDTH, PART)
    lanes = pl.ds(pl.multiple_of(info[0] * PART, PART), PART)
    for j in range(TEAM):
        for row in range(ROWS):
            joined_refs[j][row] = (raw[j][row, :, lanes].astype(F32) + branch[j, row]).astype(BF)


def upsample_kernel(info, *refs):
    parts, out = refs[:-1], refs[-1]
    wide = lax.broadcasted_iota(jnp.int32, (2 * WIDTH, WIDTH), 0) // 2
    column = lax.broadcasted_iota(jnp.int32, (2 * WIDTH, WIDTH), 1)
    twice = jnp.where(wide == column, 1.0, 0.0).astype(BF)
    for j, part in enumerate(parts):
        lanes = pl.ds(pl.multiple_of((info[0] ^ j) * PART, PART), PART)
        for row in range(ROWS):
            values = jnp.dot(twice, part[row], preferred_element_type=F32).astype(BF)
            out[2 * row, :, lanes] = values
            out[2 * row + 1, :, lanes] = values


def conv_call(kernel, name, out_shape, info, vmem_inputs, any_inputs):
    return pl.pallas_call(
        kernel,
        out_shape=out_shape,
        in_specs=[SMEM] + [VMEM] * len(vmem_inputs) + [ANY] * len(any_inputs),
        out_specs=tuple(VMEM for _ in out_shape),
        scratch_shapes=[
            pltpu.VMEM((3, TEAM, ROWS + 2, WIDTH, CH), BF),
            pltpu.VMEM((27, CH, PART), BF),
            pltpu.VMEM((3, TEAM * CELLS, PART), F32),
            pltpu.SemaphoreType.DMA((3 + 6 * TEAM,)),
        ],
        compiler_params=pltpu.CompilerParams(vmem_limit_bytes=20 * 2**20),
        cost_estimate=pl.CostEstimate(
            flops=2 * 1024 * 9 * CH * 3 * PART, bytes_accessed=12 * 10**6, transcendentals=10**6
        ),
        name=name,
    )(info, *vmem_inputs, *any_inputs)


def per_device(
    generator_latents,
    column_holder_map,
    prior_frame_index,
    caches,
    kernel_weight_pair,
    group_norm_gain,
    group_norm_shift,
):
    tile = lax.axis_index("tile")
    part = lax.axis_index("req") % TEAM
    team = range(1, TEAM)

    shard = lax.dynamic_slice_in_dim(kernel_weight_pair, part * PART, PART, axis=3)
    kernels = lax.all_gather(shard, "tile", axis=2, tiled=True)

    placed = lax.all_to_all(generator_latents, "req", split_axis=0, concat_axis=0, tiled=True)

    position = prior_frame_index[0]
    info = jnp.stack([part, tile == 0, tile == TILES - 1, position == 0]).astype(jnp.int32)

    placed, old = lax.optimization_barrier((placed, caches[0]))
    old = jnp.stack([jnp.where(position >= 2, old[:, 0], old[:, 1]), old[:, 1]], axis=1)
    old = [old] + [from_team(old, j) for j in team]
    old_edges = edges(old)

    owner = column_holder_map[0, :, 0]
    hits = (owner[:, None] == jnp.arange(TILES, dtype=jnp.int32)[None, :]).astype(jnp.int32)
    slot = jnp.sum((jnp.cumsum(hits, axis=0) - hits) * hits, axis=1)
    index = (owner * 16 + slot).astype(jnp.int32)[:, None]

    placed = lax.all_to_all(
        placed.reshape(TILES, 16, CH), "tile", split_axis=0, concat_axis=0, tiled=True
    )
    stats_shape = jax.ShapeDtypeStruct((TILES, 128), F32)
    frame, stats = pl.pallas_call(
        frame_kernel,
        out_shape=(shape(ROWS, WIDTH, CH), stats_shape),
        in_specs=[SMEM, VMEM, VMEM],
        out_specs=(VMEM, VMEM),
        compiler_params=pltpu.CompilerParams(vmem_limit_bytes=16 * 2**20),
        cost_estimate=pl.CostEstimate(flops=3 * 10**8, bytes_accessed=10**6, transcendentals=0),
        name="frame",
    )(info, index, placed)

    def exchange(values, stats):
        slots = [values] + [from_team(values, j) for j in team]
        stats = lax.all_to_all(stats, "tile", split_axis=0, concat_axis=0, tiled=True)
        slots, stats = lax.optimization_barrier((slots, stats))
        above, below = edges(slots)
        stats_team = [from_team(stats, j) for j in team]
        scales = (group_norm_gain, group_norm_shift)
        return slots, (stats, *scales, *slots, above, below, *stats_team)

    frames, inputs = exchange(frame, stats)
    hidden, first, stats = conv_call(
        conv_one_kernel,
        "conv_one",
        (shape(TEAM, ROWS, WIDTH, PART), shape(ROWS, WIDTH, CH), stats_shape),
        info,
        inputs,
        (*old, *old_edges, kernels),
    )
    _, inputs = exchange(hidden, stats)
    *joined, second = conv_call(
        conv_two_kernel,
        "conv_two",
        (shape(ROWS, WIDTH, PART),) * TEAM + (shape(ROWS, WIDTH, CH),),
        info,
        inputs + tuple(frames),
        (*old, *old_edges, kernels),
    )
    joined = [joined[0]] + [from_team(joined[j], j) for j in team]
    upsampled = pl.pallas_call(
        upsample_kernel,
        out_shape=shape(2 * ROWS, 2 * WIDTH, CH),
        in_specs=[SMEM] + [VMEM] * TEAM,
        out_specs=VMEM,
        compiler_params=pltpu.CompilerParams(vmem_limit_bytes=16 * 2**20),
        cost_estimate=pl.CostEstimate(flops=10**8, bytes_accessed=2 * 10**6, transcendentals=0),
        name="upsample",
    )(info, *joined)
    return (upsampled[None], jnp.stack([first, second])[None])


def solution(mesh):
    in_specs = (
        P(None, "req", "tile", None, None),
        P("req", None, None),
        P("req"),
        P("req", None, None, "tile", None, None),
        P(None, None, "tile", None),
        P(),
        P(),
    )
    out_specs = (P("req", "tile", None, None), P("req", None, "tile", None, None))
    return jax.shard_map(
        per_device, mesh=mesh, in_specs=in_specs, out_specs=out_specs, check_vma=False
    )
```

```python
import functools

import jax
import jax.numpy as jnp
import numpy as np
from jax import lax
from jax.experimental import pallas as pl
from jax.experimental.pallas import tpu as pltpu
from jax.sharding import PartitionSpec as P

GROUPS = 32
EPS = 1e-06
CH = 512
TEAM = 2
PART = CH // TEAM
PER = CH // GROUPS
WIDTH = 128
ROWS = 2
CELLS = ROWS * WIDTH
TILES = 32
BF, F32 = jnp.bfloat16, jnp.float32


def from_team(array, j):
    return lax.ppermute(array, "req", [(i, i ^ j) for i in range(8)])


def beside(array, step, j=0):
    perm = []
    for i in range(8):
        for t in range(TILES):
            if 0 <= t + step < TILES:
                perm.append(((i ^ j) * TILES + t + step, i * TILES + t))
    return lax.ppermute(array, ("req", "tile"), perm)


dot32 = functools.partial(jnp.dot, preferred_element_type=F32, precision=lax.Precision.HIGHEST)


def spread_lanes(channels, first_lane, transposed=False):
    shape = (128, channels) if transposed else (channels, 128)
    lane = lax.broadcasted_iota(jnp.int32, shape, 0 if transposed else 1)
    channel = lax.broadcasted_iota(jnp.int32, shape, 1 if transposed else 0)
    return jnp.where(lane == first_lane + channel // PER, 1.0, 0.0).astype(F32)


def local_stats(values):
    cells, channels = values.shape
    total = jnp.sum(values, axis=0, keepdims=True) / (cells * PER)
    mean = dot32(jnp.broadcast_to(total, (8, channels)), spread_lanes(channels, 0))
    off = values - dot32(mean, spread_lanes(channels, 0, True))[:1]
    square = jnp.broadcast_to(jnp.sum(off * off, axis=0, keepdims=True), (8, channels))
    return mean + dot32(square, spread_lanes(channels, GROUPS))


def join_stats(stats):
    lane = lax.broadcasted_iota(jnp.int32, (TILES, 128), 1)
    mean = jnp.sum(jnp.where(lane < GROUPS, stats, 0.0), axis=0, keepdims=True) / TILES
    off = jnp.where(lane < GROUPS, stats - mean, 0.0)
    between = jnp.sum(off * off, axis=0, keepdims=True) / TILES
    within = jnp.where(lane >= GROUPS, stats, 0.0)
    within = jnp.sum(within, axis=0, keepdims=True) / (TILES * CELLS * PER)
    return tuple(jnp.broadcast_to(v, (8, 128)) for v in (mean, within, between))


def norm_table(joined):
    mean, within, between = joined
    back = spread_lanes(CH, 0, True)
    spread = dot32(within, spread_lanes(CH, GROUPS, True)) + dot32(between, back)
    return dot32(mean, back)[:1], lax.rsqrt(spread[:1] + EPS)


def flagged(stats, flag):
    lane = lax.broadcasted_iota(jnp.int32, (TILES, 128), 1)
    return jnp.where(lane == 64, flag.astype(F32), jnp.broadcast_to(stats[:1], (TILES, 128)))


def flag_of(stats):
    lane = lax.broadcasted_iota(jnp.int32, (8, 128), 1)
    return jnp.max(jnp.where(lane == 64, stats[0:8, :], 0.0)) > 0.5


def silu(v):
    return v / (1.0 + jnp.exp(-v))


def norm(values, table):
    return silu((values.astype(F32) - table[0]) * table[1] + table[2]).astype(BF)


def frame_kernel(info, index_ref, placed_ref, frame_ref, last_ref, first_ref, stats_ref):
    index = index_ref[...]
    lane = lax.broadcasted_iota(jnp.int32, (WIDTH, CH), 1)
    placed = placed_ref[...].reshape(CH, CH)
    rows = []
    for row in range(ROWS):
        pick = jnp.where(lane == index + 8 * row, 1.0, 0.0).astype(BF)
        rows.append(jnp.dot(pick, placed, preferred_element_type=F32))
        frame_ref[row] = rows[row].astype(BF)
    last_ref[...] = frame_ref[ROWS - 1]
    first_ref[...] = frame_ref[0]
    stats_ref[...] = flagged(local_stats(jnp.concatenate(rows, axis=0)), info[3])


VMEM = pl.BlockSpec(memory_space=pltpu.VMEM)
SMEM = pl.BlockSpec(memory_space=pltpu.SMEM)
HBM = pl.BlockSpec(memory_space=pltpu.HBM)


def shape(*sizes):
    return jax.ShapeDtypeStruct(sizes, BF)


def start_loads(conv, kernels, inputs, earlier, raw, weights, frames, sems):
    pairs = list(zip(inputs, raw)) + [(earlier[j], frames.at[pl.ds(0, 2), j]) for j in range(TEAM)]
    copies = [pltpu.make_async_copy(src, dst, sems.at[3 + k]) for k, (src, dst) in enumerate(pairs)]
    for copy in copies:
        copy.start()
    for a in range(3):
        part = pl.ds(9 * a, 9)
        pltpu.make_async_copy(kernels.at[conv, part], weights.at[part], sems.at[a]).start()
    for copy in copies[: len(inputs)]:
        copy.wait()
    return copies[len(inputs) :]


def finish_history(parts, copies, frames):
    for copy in copies:
        copy.wait()
    for j, part in enumerate(parts):

        @pl.when(flag_of(part))
        def _():
            for row in range(ROWS + 2):
                frames[0, j, row] = frames[2, j, row]
                frames[1, j, row] = frames[2, j, row]


def convolve(frames, weights, sems, acc):
    cells = TEAM * CELLS
    for a in range(3):
        part = weights.at[pl.ds(9 * a, 9)]
        pltpu.make_async_copy(part, part, sems.at[a]).wait()
        for b in range(3):
            slab = frames[a, :, pl.ds(b, ROWS)].reshape(cells, CH)
            for c in range(3):
                tap = weights[9 * a + 3 * b + c]
                product = jnp.dot(slab, tap, preferred_element_type=F32)
                if a == 0 and b == 0:
                    acc[c] = product
                else:
                    acc[c] += product
    column = lax.broadcasted_iota(jnp.int32, (cells, PART), 0) % WIDTH
    left = jnp.where(column == 0, 0.0, pltpu.roll(acc[0], 1, 0))
    right = jnp.where(column == WIDTH - 1, 0.0, pltpu.roll(acc[2], cells - 1, 0))
    return acc[1] + left + right


def split(refs, *sizes):
    ends = np.cumsum((0,) + sizes)
    return [refs[a:b] for a, b in zip(ends[:-1], ends[1:])]


def first_kernel(info, stats, gain, shift, *refs):
    values, above, below, (out,) = split(refs, TEAM, TEAM, TEAM, 1)
    zeros = jnp.zeros((WIDTH, CH), BF)
    for j, frame in enumerate(values):
        mean, scale = norm_table(join_stats(stats[:, 128 * j : 128 * j + 128]))
        table = (mean, scale * gain[0:1, :], shift[0:1, :])
        for row in range(ROWS):
            out[j, 1 + row] = norm(frame[row], table)
        out[j, 0] = jnp.where(info[1] == 1, zeros, norm(above[j][...], table))
        out[j, ROWS + 1] = jnp.where(info[2] == 1, zeros, norm(below[j][...], table))


def conv_one_kernel(info, gain, shift, *refs):
    (stats,), inputs, earlier, (kernels,), outs, scratch = split(refs, 1, 1, TEAM, 1, 5, 4)
    hidden_ref, last_ref, top_ref, first_ref, stats_ref = outs
    frames, weights, acc, sems = scratch
    parts = [stats[:, 128 * j : 128 * j + 128] for j in range(TEAM)]
    copies = start_loads(0, kernels, inputs, earlier, [frames.at[2]], weights, frames, sems)
    for row in range(ROWS):
        first_ref[row] = frames[2, 0, 1 + row]
    finish_history(parts, copies, frames)
    total = convolve(frames, weights, sems, acc).astype(BF)
    hidden_ref[...] = total.reshape(TEAM, ROWS, WIDTH, PART)
    for j in range(TEAM):
        last_ref[j] = hidden_ref[j, ROWS - 1]
        top_ref[j] = hidden_ref[j, 0]
    total = total.astype(F32)
    total = jnp.concatenate([total[j * CELLS : (j + 1) * CELLS] for j in range(TEAM)], axis=1)
    stats_ref[...] = flagged(local_stats(total), info[3])


def conv_two_kernel(info, gain, shift, *refs):
    (stats,), inputs, residual, earlier, (kernels,), outs, raw, scratch = split(
        refs, 1, TEAM, TEAM, TEAM, 1, TEAM + 1, 2 * TEAM, 4
    )
    frames, weights, acc, sems = scratch
    copies = start_loads(1, kernels, inputs + residual, earlier, raw, weights, frames, sems)
    parts = [stats[:, 128 * j : 128 * j + 128] for j in range(TEAM)]
    values, residual = split(raw, TEAM, TEAM)
    zeros = jnp.zeros((WIDTH, PART), BF)
    for k, (hidden, part) in enumerate(zip(values, parts)):
        mean, scale = norm_table(join_stats(part))
        lanes = pl.ds(pl.multiple_of((info[0] ^ k) * PART, PART), PART)
        gains, shifts = gain[1:2, lanes], shift[1:2, lanes]
        for j in range(TEAM):
            here = slice((j ^ k) * PART, (j ^ k) * PART + PART)
            table = (mean[:, here], scale[:, here] * gains, shifts)
            for row in range(ROWS + 2):
                values_row = norm(hidden[j ^ k, row], table)
                if row == 0:
                    values_row = jnp.where(info[1] == 1, zeros, values_row)
                elif row == ROWS + 1:
                    values_row = jnp.where(info[2] == 1, zeros, values_row)
                frames[2, j, row, :, lanes] = values_row
    for row in range(ROWS):
        outs[TEAM][row] = frames[2, 0, 1 + row]
    finish_history(parts, copies, frames)
    branch = convolve(frames, weights, sems, acc).reshape(TEAM, ROWS, WIDTH, PART)
    lanes = pl.ds(pl.multiple_of(info[0] * PART, PART), PART)
    for j in range(TEAM):
        for row in range(ROWS):
            joined = residual[j][row, :, lanes].astype(F32) + branch[j, row]
            outs[j][row] = joined.astype(BF)


def upsample_kernel(info, *refs):
    parts, out = refs[:-1], refs[-1]
    wide = lax.broadcasted_iota(jnp.int32, (2 * WIDTH, WIDTH), 0) // 2
    column = lax.broadcasted_iota(jnp.int32, (2 * WIDTH, WIDTH), 1)
    twice = jnp.where(wide == column, 1.0, 0.0).astype(BF)
    for j, part in enumerate(parts):
        lanes = pl.ds(pl.multiple_of((info[0] ^ j) * PART, PART), PART)
        for row in range(ROWS):
            values = jnp.dot(twice, part[row], preferred_element_type=F32).astype(BF)
            out[2 * row, :, lanes] = values
            out[2 * row + 1, :, lanes] = values


def conv_call(kernel, name, out_shape, info, scales, stats, inputs, earlier, kernels, raw):
    return pl.pallas_call(
        kernel,
        out_shape=out_shape,
        in_specs=[SMEM] + [VMEM] * 3 + [HBM] * (len(inputs) + TEAM + 1),
        out_specs=tuple(VMEM for _ in out_shape),
        scratch_shapes=[pltpu.VMEM(array.shape, BF) for array in inputs[:raw]]
        + [
            pltpu.VMEM((3, TEAM, ROWS + 2, WIDTH, CH), BF),
            pltpu.VMEM((27, CH, PART), BF),
            pltpu.VMEM((3, TEAM * CELLS, PART), F32),
            pltpu.SemaphoreType.DMA((3 + len(inputs) + TEAM,)),
        ],
        compiler_params=pltpu.CompilerParams(vmem_limit_bytes=50 * 2**20),
        cost_estimate=pl.CostEstimate(
            flops=2 * 512 * 27 * CH * PART, bytes_accessed=12 * 10**6, transcendentals=10**6
        ),
        name=name,
    )(info, *scales, stats, *inputs, *earlier, kernels)


def per_device(
    generator_latents,
    column_holder_map,
    prior_frame_index,
    caches,
    kernel_weight_pair,
    group_norm_gain,
    group_norm_shift,
):
    tile = lax.axis_index("tile")
    part = lax.axis_index("req") % TEAM
    team = range(1, TEAM)

    shard = lax.dynamic_slice_in_dim(kernel_weight_pair, part * PART, PART, axis=3)
    kernels = lax.all_gather(shard, "tile", axis=2, tiled=True)

    placed = lax.all_to_all(generator_latents, "req", split_axis=0, concat_axis=0, tiled=True)

    position = prior_frame_index[0]
    info = jnp.stack([part, tile == 0, tile == TILES - 1, position == 0]).astype(jnp.int32)

    def history(rows):
        return jnp.stack([jnp.where(position >= 2, rows[:, 0], rows[:, 1]), rows[:, 1]], axis=1)

    above = beside(history(caches[0, :, :, ROWS - 1]), -1)
    below = beside(history(caches[0, :, :, 0]), 1)
    placed, above, below, earlier = lax.optimization_barrier((placed, above, below, caches[0]))
    earlier = history(earlier)


    def of_team(own):
        return [own] + [from_team(own, j) for j in team]

    old = [
        jnp.concatenate([above[conv][:, None], earlier[conv], below[conv][:, None]], axis=1)
        for conv in range(2)
    ]
    placed, old = lax.optimization_barrier((placed, old))
    old_one = of_team(old[0])

    owner = column_holder_map[0, :, 0]
    hits = (owner[:, None] == jnp.arange(TILES, dtype=jnp.int32)[None, :]).astype(jnp.int32)
    slot = jnp.sum((jnp.cumsum(hits, axis=0) - hits) * hits, axis=1)
    index = (owner * 16 + slot).astype(jnp.int32)[:, None]

    placed = lax.all_to_all(
        placed.reshape(TILES, 16, CH), "tile", split_axis=0, concat_axis=0, tiled=True
    )
    stats_shape = jax.ShapeDtypeStruct((TILES, 128), F32)
    frame, last, top, stats = pl.pallas_call(
        frame_kernel,
        out_shape=(shape(ROWS, WIDTH, CH), shape(WIDTH, CH), shape(WIDTH, CH), stats_shape),
        in_specs=[SMEM, VMEM, VMEM],
        out_specs=(VMEM, VMEM, VMEM, VMEM),
        compiler_params=pltpu.CompilerParams(vmem_limit_bytes=16 * 2**20),
        cost_estimate=pl.CostEstimate(flops=3 * 10**8, bytes_accessed=10**6, transcendentals=0),
        name="frame",
    )(info, index, placed)

    def exchange(values, last, top, stats):
        slots = [values] + [from_team(values, j) for j in team]
        above = [beside(last, -1, j) for j in range(TEAM)]
        below = [beside(top, 1, j) for j in range(TEAM)]
        stats = jnp.concatenate([stats] + [from_team(stats, j) for j in team], axis=1)
        stats = lax.all_to_all(stats, "tile", split_axis=0, concat_axis=0, tiled=True)
        return slots, stats, [*slots, *above, *below]

    scales = (group_norm_gain, group_norm_shift)
    frames, stats, inputs = exchange(frame, last, top, stats)
    inputs, late = lax.optimization_barrier((inputs, old[1]))
    old_two = of_team(late)
    current = pl.pallas_call(
        first_kernel,
        out_shape=shape(TEAM, ROWS + 2, WIDTH, CH),
        in_specs=[SMEM] + [VMEM] * (3 + len(inputs)),
        out_specs=VMEM,
        compiler_params=pltpu.CompilerParams(vmem_limit_bytes=16 * 2**20),
        cost_estimate=pl.CostEstimate(
            flops=10**7, bytes_accessed=3 * 10**6, transcendentals=10**6
        ),
        name="first",
    )(info, stats, *scales, *inputs)
    hidden, last, top, first, stats = conv_call(
        conv_one_kernel,
        "conv_one",
        (shape(TEAM, ROWS, WIDTH, PART),)
        + (shape(TEAM, WIDTH, PART),) * 2
        + (shape(ROWS, WIDTH, CH), stats_shape),
        info,
        scales,
        stats,
        [current],
        old_one,
        kernels,
        0,
    )
    above, below = beside(last, -1), beside(top, 1)
    stats = jnp.concatenate([stats] + [from_team(stats, j) for j in team], axis=1)
    above, below, stats = lax.optimization_barrier((above, below, stats))
    current = jnp.concatenate([above[:, None], hidden, below[:, None]], axis=1)
    inputs = [current] + [from_team(current, j) for j in team]
    stats = lax.all_to_all(stats, "tile", split_axis=0, concat_axis=0, tiled=True)
    *joined, second = conv_call(
        conv_two_kernel,
        "conv_two",
        (shape(ROWS, WIDTH, PART),) * TEAM + (shape(ROWS, WIDTH, CH),),
        info,
        scales,
        stats,
        inputs + frames,
        old_two,
        kernels,
        2 * TEAM,
    )
    joined = [joined[0]] + [from_team(joined[j], j) for j in team]
    upsampled = pl.pallas_call(
        upsample_kernel,
        out_shape=shape(2 * ROWS, 2 * WIDTH, CH),
        in_specs=[SMEM] + [VMEM] * TEAM,
        out_specs=VMEM,
        compiler_params=pltpu.CompilerParams(vmem_limit_bytes=16 * 2**20),
        cost_estimate=pl.CostEstimate(flops=10**8, bytes_accessed=2 * 10**6, transcendentals=0),
        name="upsample",
    )(info, *joined)
    return (upsampled[None], jnp.stack([first, second])[None])


def solution(mesh):
    in_specs = (
        P(None, "req", "tile", None, None),
        P("req", None, None),
        P("req"),
        P("req", None, None, "tile", None, None),
        P(None, None, "tile", None),
        P(),
        P(),
    )
    out_specs = (P("req", "tile", None, None), P("req", None, "tile", None, None))
    return jax.shard_map(
        per_device, mesh=mesh, in_specs=in_specs, out_specs=out_specs, check_vma=False
    )
```

```python
import functools

import jax
import jax.numpy as jnp
import numpy as np
from jax import lax
from jax.experimental import pallas as pl
from jax.experimental.pallas import tpu as pltpu
from jax.sharding import PartitionSpec as P

GROUPS = 32
EPS = 1e-06
CH = 512
TEAM = 2
PART = CH // TEAM
PER = CH // GROUPS
WIDTH = 128
ROWS = 2
CELLS = ROWS * WIDTH
TILES = 32
BF, F32 = jnp.bfloat16, jnp.float32


def from_team(array, j):
    return lax.ppermute(array, "req", [(i, i ^ j) for i in range(8)])


def beside(array, step, j=0):
    perm = []
    for i in range(8):
        for t in range(TILES):
            if 0 <= t + step < TILES:
                perm.append(((i ^ j) * TILES + t + step, i * TILES + t))
    return lax.ppermute(array, ("req", "tile"), perm)


dot32 = functools.partial(jnp.dot, preferred_element_type=F32, precision=lax.Precision.HIGHEST)


def spread_lanes(channels, first_lane, transposed=False):
    shape = (128, channels) if transposed else (channels, 128)
    lane = lax.broadcasted_iota(jnp.int32, shape, 0 if transposed else 1)
    channel = lax.broadcasted_iota(jnp.int32, shape, 1 if transposed else 0)
    return jnp.where(lane == first_lane + channel // PER, 1.0, 0.0).astype(F32)


def local_stats(values):
    cells, channels = values.shape
    total = jnp.sum(values, axis=0, keepdims=True) / (cells * PER)
    mean = dot32(jnp.broadcast_to(total, (8, channels)), spread_lanes(channels, 0))
    off = values - dot32(mean, spread_lanes(channels, 0, True))[:1]
    square = jnp.broadcast_to(jnp.sum(off * off, axis=0, keepdims=True), (8, channels))
    return mean + dot32(square, spread_lanes(channels, GROUPS))


def join_stats(stats):
    lane = lax.broadcasted_iota(jnp.int32, (TILES, 128), 1)
    mean = jnp.sum(jnp.where(lane < GROUPS, stats, 0.0), axis=0, keepdims=True) / TILES
    off = jnp.where(lane < GROUPS, stats - mean, 0.0)
    between = jnp.sum(off * off, axis=0, keepdims=True) / TILES
    within = jnp.where(lane >= GROUPS, stats, 0.0)
    within = jnp.sum(within, axis=0, keepdims=True) / (TILES * CELLS * PER)
    return tuple(jnp.broadcast_to(v, (8, 128)) for v in (mean, within, between))


def norm_table(joined):
    mean, within, between = joined
    back = spread_lanes(CH, 0, True)
    spread = dot32(within, spread_lanes(CH, GROUPS, True)) + dot32(between, back)
    return dot32(mean, back)[:1], lax.rsqrt(spread[:1] + EPS)


def flagged(stats, flag):
    lane = lax.broadcasted_iota(jnp.int32, (TILES, 128), 1)
    return jnp.where(lane == 64, flag.astype(F32), jnp.broadcast_to(stats[:1], (TILES, 128)))


def flag_of(stats):
    lane = lax.broadcasted_iota(jnp.int32, (8, 128), 1)
    return jnp.max(jnp.where(lane == 64, stats[0:8, :], 0.0)) > 0.5


def silu(v):
    return v / (1.0 + jnp.exp(-v))


def norm(values, table):
    return silu((values.astype(F32) - table[0]) * table[1] + table[2]).astype(BF)


def frame_kernel(info, index_ref, placed_ref, frame_ref, last_ref, first_ref, stats_ref):
    index = index_ref[...]
    lane = lax.broadcasted_iota(jnp.int32, (WIDTH, CH), 1)
    placed = placed_ref[...].reshape(CH, CH)
    rows = []
    for row in range(ROWS):
        pick = jnp.where(lane == index + 8 * row, 1.0, 0.0).astype(BF)
        rows.append(jnp.dot(pick, placed, preferred_element_type=F32))
        frame_ref[row] = rows[row].astype(BF)
    last_ref[...] = frame_ref[ROWS - 1]
    first_ref[...] = frame_ref[0]
    stats_ref[...] = flagged(local_stats(jnp.concatenate(rows, axis=0)), info[3])


VMEM = pl.BlockSpec(memory_space=pltpu.VMEM)
SMEM = pl.BlockSpec(memory_space=pltpu.SMEM)
HBM = pl.BlockSpec(memory_space=pltpu.HBM)


def shape(*sizes):
    return jax.ShapeDtypeStruct(sizes, BF)


def start_loads(conv, kernels, inputs, earlier, raw, weights, frames, sems):
    pairs = list(zip(inputs, raw)) + [(earlier[j], frames.at[pl.ds(0, 2), j]) for j in range(TEAM)]
    copies = [pltpu.make_async_copy(src, dst, sems.at[9 + k]) for k, (src, dst) in enumerate(pairs)]
    for copy in copies:
        copy.start()
    for k in range(9):
        part = pl.ds(3 * k, 3)
        pltpu.make_async_copy(kernels.at[conv, part], weights.at[part], sems.at[k]).start()
    for copy in copies[: len(inputs)]:
        copy.wait()
    return copies[len(inputs) :]


def finish_history(parts, copies, frames):
    for copy in copies:
        copy.wait()
    for j, part in enumerate(parts):

        @pl.when(flag_of(part))
        def _():
            for row in range(ROWS + 2):
                frames[0, j, row] = frames[2, j, row]
                frames[1, j, row] = frames[2, j, row]


def convolve(frames, weights, sems, acc):
    cells = TEAM * CELLS
    for a in range(3):
        for b in range(3):
            part = weights.at[pl.ds(9 * a + 3 * b, 3)]
            pltpu.make_async_copy(part, part, sems.at[3 * a + b]).wait()
        for j in range(TEAM):
            here = pl.ds(j * CELLS, CELLS)
            for c in range(3):
                total = acc[c, here] if a else None
                for b in range(3):
                    slab = frames[a, j, pl.ds(b, ROWS)].reshape(CELLS, CH)
                    tap = weights[9 * a + 3 * b + c]
                    product = jnp.dot(slab, tap, preferred_element_type=F32)
                    total = product if total is None else total + product
                acc[c, here] = total
    column = lax.broadcasted_iota(jnp.int32, (cells, PART), 0) % WIDTH
    left = jnp.where(column == 0, 0.0, pltpu.roll(acc[0], 1, 0))
    right = jnp.where(column == WIDTH - 1, 0.0, pltpu.roll(acc[2], cells - 1, 0))
    return acc[1] + left + right


def split(refs, *sizes):
    ends = np.cumsum((0,) + sizes)
    return [refs[a:b] for a, b in zip(ends[:-1], ends[1:])]


def first_kernel(info, stats, gain, shift, *refs):
    values, above, below, (out, first_ref) = split(refs, TEAM, TEAM, TEAM, 2)
    zeros = jnp.zeros((WIDTH, CH), BF)
    for j, frame in enumerate(values):
        mean, scale = norm_table(join_stats(stats[:, 128 * j : 128 * j + 128]))
        table = (mean, scale * gain[0:1, :], shift[0:1, :])
        for row in range(ROWS):
            out[j, 1 + row] = norm(frame[row], table)
            if j == 0:
                first_ref[row] = out[0, 1 + row]
        out[j, 0] = jnp.where(info[1] == 1, zeros, norm(above[j][...], table))
        out[j, ROWS + 1] = jnp.where(info[2] == 1, zeros, norm(below[j][...], table))


def conv_one_kernel(info, gain, shift, *refs):
    (stats,), inputs, earlier, (kernels,), outs, scratch = split(refs, 1, 1, TEAM, 1, 4, 4)
    hidden_ref, last_ref, top_ref, stats_ref = outs
    frames, weights, acc, sems = scratch
    parts = [stats[:, 128 * j : 128 * j + 128] for j in range(TEAM)]
    copies = start_loads(0, kernels, inputs, earlier, [frames.at[2]], weights, frames, sems)
    finish_history(parts, copies, frames)
    total = convolve(frames, weights, sems, acc).astype(BF)
    hidden_ref[...] = total.reshape(TEAM, ROWS, WIDTH, PART)
    for j in range(TEAM):
        last_ref[j] = hidden_ref[j, ROWS - 1]
        top_ref[j] = hidden_ref[j, 0]
    total = total.astype(F32)
    total = jnp.concatenate([total[j * CELLS : (j + 1) * CELLS] for j in range(TEAM)], axis=1)
    stats_ref[...] = flagged(local_stats(total), info[3])


def conv_two_kernel(info, gain, shift, *refs):
    (stats,), inputs, residual, earlier, (kernels,), outs, raw, scratch = split(
        refs, 1, TEAM, TEAM, TEAM, 1, TEAM + 1, 2 * TEAM, 4
    )
    frames, weights, acc, sems = scratch
    copies = start_loads(1, kernels, inputs + residual, earlier, raw, weights, frames, sems)
    parts = [stats[:, 128 * j : 128 * j + 128] for j in range(TEAM)]
    values, residual = split(raw, TEAM, TEAM)
    zeros = jnp.zeros((WIDTH, PART), BF)
    for k, (hidden, part) in enumerate(zip(values, parts)):
        mean, scale = norm_table(join_stats(part))
        lanes = pl.ds(pl.multiple_of((info[0] ^ k) * PART, PART), PART)
        gains, shifts = gain[1:2, lanes], shift[1:2, lanes]
        for j in range(TEAM):
            here = slice((j ^ k) * PART, (j ^ k) * PART + PART)
            table = (mean[:, here], scale[:, here] * gains, shifts)
            for row in range(ROWS + 2):
                values_row = norm(hidden[j ^ k, row], table)
                if row == 0:
                    values_row = jnp.where(info[1] == 1, zeros, values_row)
                elif row == ROWS + 1:
                    values_row = jnp.where(info[2] == 1, zeros, values_row)
                frames[2, j, row, :, lanes] = values_row
    for row in range(ROWS):
        outs[TEAM][row] = frames[2, 0, 1 + row]
    finish_history(parts, copies, frames)
    branch = convolve(frames, weights, sems, acc).reshape(TEAM, ROWS, WIDTH, PART)
    lanes = pl.ds(pl.multiple_of(info[0] * PART, PART), PART)
    for j in range(TEAM):
        for row in range(ROWS):
            joined = residual[j][row, :, lanes].astype(F32) + branch[j, row]
            outs[j][row] = joined.astype(BF)


def upsample_kernel(info, *refs):
    parts, out = refs[:-1], refs[-1]
    wide = lax.broadcasted_iota(jnp.int32, (2 * WIDTH, WIDTH), 0) // 2
    column = lax.broadcasted_iota(jnp.int32, (2 * WIDTH, WIDTH), 1)
    twice = jnp.where(wide == column, 1.0, 0.0).astype(BF)
    for j, part in enumerate(parts):
        lanes = pl.ds(pl.multiple_of((info[0] ^ j) * PART, PART), PART)
        for row in range(ROWS):
            values = jnp.dot(twice, part[row], preferred_element_type=F32).astype(BF)
            out[2 * row, :, lanes] = values
            out[2 * row + 1, :, lanes] = values


def conv_call(kernel, name, out_shape, info, scales, stats, inputs, earlier, kernels, raw):
    return pl.pallas_call(
        kernel,
        out_shape=out_shape,
        in_specs=[SMEM] + [VMEM] * 3 + [HBM] * (len(inputs) + TEAM + 1),
        out_specs=tuple(VMEM for _ in out_shape),
        scratch_shapes=[pltpu.VMEM(array.shape, BF) for array in inputs[:raw]]
        + [
            pltpu.VMEM((3, TEAM, ROWS + 2, WIDTH, CH), BF),
            pltpu.VMEM((27, CH, PART), BF),
            pltpu.VMEM((3, TEAM * CELLS, PART), F32),
            pltpu.SemaphoreType.DMA((9 + len(inputs) + TEAM,)),
        ],
        compiler_params=pltpu.CompilerParams(vmem_limit_bytes=50 * 2**20),
        cost_estimate=pl.CostEstimate(
            flops=2 * 512 * 27 * CH * PART, bytes_accessed=12 * 10**6, transcendentals=10**6
        ),
        name=name,
    )(info, *scales, stats, *inputs, *earlier, kernels)


def per_device(
    generator_latents,
    column_holder_map,
    prior_frame_index,
    caches,
    kernel_weight_pair,
    group_norm_gain,
    group_norm_shift,
):
    tile = lax.axis_index("tile")
    part = lax.axis_index("req") % TEAM
    team = range(1, TEAM)

    shard = lax.dynamic_slice_in_dim(kernel_weight_pair, part * PART, PART, axis=3)
    kernels = lax.all_gather(shard, "tile", axis=2, tiled=True)

    placed = lax.all_to_all(generator_latents, "req", split_axis=0, concat_axis=0, tiled=True)

    position = prior_frame_index[0]
    info = jnp.stack([part, tile == 0, tile == TILES - 1, position == 0]).astype(jnp.int32)

    def history(rows):
        return jnp.stack([jnp.where(position >= 2, rows[:, 0], rows[:, 1]), rows[:, 1]], axis=1)

    above = beside(history(caches[0, :, :, ROWS - 1]), -1)
    below = beside(history(caches[0, :, :, 0]), 1)
    placed, above, below, earlier = lax.optimization_barrier((placed, above, below, caches[0]))
    earlier = history(earlier)


    def of_team(own):
        return [own] + [from_team(own, j) for j in team]

    old = [
        jnp.concatenate([above[conv][:, None], earlier[conv], below[conv][:, None]], axis=1)
        for conv in range(2)
    ]
    placed, old = lax.optimization_barrier((placed, old))
    old_one = of_team(old[0])

    owner = column_holder_map[0, :, 0]
    hits = (owner[:, None] == jnp.arange(TILES, dtype=jnp.int32)[None, :]).astype(jnp.int32)
    slot = jnp.sum((jnp.cumsum(hits, axis=0) - hits) * hits, axis=1)
    index = (owner * 16 + slot).astype(jnp.int32)[:, None]

    placed = lax.all_to_all(
        placed.reshape(TILES, 16, CH), "tile", split_axis=0, concat_axis=0, tiled=True
    )
    stats_shape = jax.ShapeDtypeStruct((TILES, 128), F32)
    frame, last, top, stats = pl.pallas_call(
        frame_kernel,
        out_shape=(shape(ROWS, WIDTH, CH), shape(WIDTH, CH), shape(WIDTH, CH), stats_shape),
        in_specs=[SMEM, VMEM, VMEM],
        out_specs=(VMEM, VMEM, VMEM, VMEM),
        compiler_params=pltpu.CompilerParams(vmem_limit_bytes=16 * 2**20),
        cost_estimate=pl.CostEstimate(flops=3 * 10**8, bytes_accessed=10**6, transcendentals=0),
        name="frame",
    )(info, index, placed)

    def exchange(values, last, top, stats):
        slots = [values] + [from_team(values, j) for j in team]
        above = [beside(last, -1, j) for j in range(TEAM)]
        below = [beside(top, 1, j) for j in range(TEAM)]
        stats = jnp.concatenate([stats] + [from_team(stats, j) for j in team], axis=1)
        stats = lax.all_to_all(stats, "tile", split_axis=0, concat_axis=0, tiled=True)
        return slots, stats, [*slots, *above, *below]

    scales = (group_norm_gain, group_norm_shift)
    frames, stats, inputs = exchange(frame, last, top, stats)
    inputs, late = lax.optimization_barrier((inputs, old[1]))
    old_two = of_team(late)
    current, first = pl.pallas_call(
        first_kernel,
        out_shape=(shape(TEAM, ROWS + 2, WIDTH, CH), shape(ROWS, WIDTH, CH)),
        in_specs=[SMEM] + [VMEM] * (3 + len(inputs)),
        out_specs=(VMEM, VMEM),
        compiler_params=pltpu.CompilerParams(vmem_limit_bytes=16 * 2**20),
        cost_estimate=pl.CostEstimate(
            flops=10**7, bytes_accessed=3 * 10**6, transcendentals=10**6
        ),
        name="first",
    )(info, stats, *scales, *inputs)
    hidden, last, top, stats = conv_call(
        conv_one_kernel,
        "conv_one",
        (shape(TEAM, ROWS, WIDTH, PART),)
        + (shape(TEAM, WIDTH, PART),) * 2
        + (stats_shape,),
        info,
        scales,
        stats,
        [current],
        old_one,
        kernels,
        0,
    )
    above, below = beside(last, -1), beside(top, 1)
    stats = jnp.concatenate([stats] + [from_team(stats, j) for j in team], axis=1)
    above, below, stats = lax.optimization_barrier((above, below, stats))
    current = jnp.concatenate([above[:, None], hidden, below[:, None]], axis=1)
    inputs = [current] + [from_team(current, j) for j in team]
    stats = lax.all_to_all(stats, "tile", split_axis=0, concat_axis=0, tiled=True)
    *joined, second = conv_call(
        conv_two_kernel,
        "conv_two",
        (shape(ROWS, WIDTH, PART),) * TEAM + (shape(ROWS, WIDTH, CH),),
        info,
        scales,
        stats,
        inputs + frames,
        old_two,
        kernels,
        2 * TEAM,
    )
    joined = [joined[0]] + [from_team(joined[j], j) for j in team]
    upsampled = pl.pallas_call(
        upsample_kernel,
        out_shape=shape(2 * ROWS, 2 * WIDTH, CH),
        in_specs=[SMEM] + [VMEM] * TEAM,
        out_specs=VMEM,
        compiler_params=pltpu.CompilerParams(vmem_limit_bytes=16 * 2**20),
        cost_estimate=pl.CostEstimate(flops=10**8, bytes_accessed=2 * 10**6, transcendentals=0),
        name="upsample",
    )(info, *joined)
    return (upsampled[None], jnp.stack([first, second])[None])


def solution(mesh):
    in_specs = (
        P(None, "req", "tile", None, None),
        P("req", None, None),
        P("req"),
        P("req", None, None, "tile", None, None),
        P(None, None, "tile", None),
        P(),
        P(),
    )
    out_specs = (P("req", "tile", None, None), P("req", None, "tile", None, None))
    return jax.shard_map(
        per_device, mesh=mesh, in_specs=in_specs, out_specs=out_specs, check_vma=False
    )
```

```python
import functools

import jax
import jax.numpy as jnp
import numpy as np
from jax import lax
from jax.experimental import pallas as pl
from jax.experimental.pallas import tpu as pltpu
from jax.sharding import PartitionSpec as P

GROUPS = 32
EPS = 1e-06
CH = 512
TEAM = 2
PART = CH // TEAM
PER = CH // GROUPS
WIDTH = 128
ROWS = 2
CELLS = ROWS * WIDTH
TILES = 32
HELD = 16
TAP_ORDER = (2, 0, 1)
BF, F32 = jnp.bfloat16, jnp.float32


def from_team(array, j):
    return lax.ppermute(array, "req", [(i, i ^ j) for i in range(8)])


def beside(array, step, j=0):
    perm = []
    for i in range(8):
        for t in range(TILES):
            if 0 <= t + step < TILES:
                perm.append(((i ^ j) * TILES + t + step, i * TILES + t))
    return lax.ppermute(array, ("req", "tile"), perm)


dot32 = functools.partial(jnp.dot, preferred_element_type=F32, precision=lax.Precision.HIGHEST)


def spread_lanes(channels, first_lane, transposed=False):
    shape = (128, channels) if transposed else (channels, 128)
    lane = lax.broadcasted_iota(jnp.int32, shape, 0 if transposed else 1)
    channel = lax.broadcasted_iota(jnp.int32, shape, 1 if transposed else 0)
    return jnp.where(lane == first_lane + channel // PER, 1.0, 0.0).astype(F32)


def local_stats(values):
    cells, channels = values.shape
    total = jnp.sum(values, axis=0, keepdims=True) / (cells * PER)
    mean = dot32(jnp.broadcast_to(total, (8, channels)), spread_lanes(channels, 0))
    off = values - dot32(mean, spread_lanes(channels, 0, True))[:1]
    square = jnp.broadcast_to(jnp.sum(off * off, axis=0, keepdims=True), (8, channels))
    return mean + dot32(square, spread_lanes(channels, GROUPS))


def join_stats(stats):
    lane = lax.broadcasted_iota(jnp.int32, (TILES, 128), 1)
    mean = jnp.sum(jnp.where(lane < GROUPS, stats, 0.0), axis=0, keepdims=True) / TILES
    off = jnp.where(lane < GROUPS, stats - mean, 0.0)
    between = jnp.sum(off * off, axis=0, keepdims=True) / TILES
    within = jnp.where(lane >= GROUPS, stats, 0.0)
    within = jnp.sum(within, axis=0, keepdims=True) / (TILES * CELLS * PER)
    return tuple(jnp.broadcast_to(v, (8, 128)) for v in (mean, within, between))


def norm_table(joined):
    mean, within, between = joined
    back = spread_lanes(CH, 0, True)
    spread = dot32(within, spread_lanes(CH, GROUPS, True)) + dot32(between, back)
    return dot32(mean, back)[:1], lax.rsqrt(spread[:1] + EPS)


def flagged(stats, flag):
    lane = lax.broadcasted_iota(jnp.int32, (TILES, 128), 1)
    return jnp.where(lane == 64, flag.astype(F32), jnp.broadcast_to(stats[:1], (TILES, 128)))


def flag_of(stats):
    lane = lax.broadcasted_iota(jnp.int32, (8, 128), 1)
    return jnp.max(jnp.where(lane == 64, stats[0:8, :], 0.0)) > 0.5


def silu(v):
    return v / (1.0 + jnp.exp(-v))


def norm(values, table):
    return silu((values.astype(F32) - table[0]) * table[1] + table[2]).astype(BF)


def frame_kernel(info, index_ref, placed_ref, frame_ref, last_ref, first_ref, stats_ref):
    index = index_ref[...]
    lane = lax.broadcasted_iota(jnp.int32, (WIDTH, CH), 1)
    placed = placed_ref[...].reshape(CH, CH)
    rows = []
    for row in range(ROWS):
        pick = jnp.where(lane == index + 8 * row, 1.0, 0.0).astype(BF)
        rows.append(jnp.dot(pick, placed, preferred_element_type=F32))
        frame_ref[row] = rows[row].astype(BF)
    last_ref[...] = frame_ref[ROWS - 1]
    first_ref[...] = frame_ref[0]
    stats_ref[...] = flagged(local_stats(jnp.concatenate(rows, axis=0)), info[3])


VMEM = pl.BlockSpec(memory_space=pltpu.VMEM)
SMEM = pl.BlockSpec(memory_space=pltpu.SMEM)
HBM = pl.BlockSpec(memory_space=pltpu.HBM)


def shape(*sizes):
    return jax.ShapeDtypeStruct(sizes, BF)


def start_loads(conv, kernels, inputs, earlier, raw, weights, frames, sems):
    pairs = list(zip(inputs, raw)) + [(earlier[j], frames.at[pl.ds(0, 2), j]) for j in range(TEAM)]
    copies = [pltpu.make_async_copy(src, dst, sems.at[9 + k]) for k, (src, dst) in enumerate(pairs)]
    first, later = copies[: len(inputs)], copies[len(inputs) :]
    for copy in first:
        copy.start()
    for a in TAP_ORDER:
        for b in range(3):
            part = pl.ds(9 * a + 3 * b, 3)
            sem = sems.at[3 * a + b]
            pltpu.make_async_copy(kernels.at[conv, part], weights.at[part], sem).start()
        for copy in later if a == 2 else ():
            copy.start()
    for copy in first:
        copy.wait()
    return later


def finish_history(parts, copies, frames):
    for copy in copies:
        copy.wait()
    for j, part in enumerate(parts):

        @pl.when(flag_of(part))
        def _():
            for row in range(ROWS + 2):
                frames[0, j, row] = frames[2, j, row]
                frames[1, j, row] = frames[2, j, row]


def convolve(parts, copies, frames, weights, sems, acc):
    cells = TEAM * CELLS
    for a in TAP_ORDER:
        if a == 0:
            finish_history(parts, copies, frames)
        for b in range(3):
            part = weights.at[pl.ds(9 * a + 3 * b, 3)]
            pltpu.make_async_copy(part, part, sems.at[3 * a + b]).wait()
        for j in range(TEAM):
            here = pl.ds(j * CELLS, CELLS)
            for c in range(3):
                total = None if a == 2 else acc[c, here]
                for b in range(3):
                    slab = frames[a, j, pl.ds(b, ROWS)].reshape(CELLS, CH)
                    tap = weights[9 * a + 3 * b + c]
                    product = jnp.dot(slab, tap, preferred_element_type=F32)
                    total = product if total is None else total + product
                acc[c, here] = total
    column = lax.broadcasted_iota(jnp.int32, (cells, PART), 0) % WIDTH
    left = jnp.where(column == 0, 0.0, pltpu.roll(acc[0], 1, 0))
    right = jnp.where(column == WIDTH - 1, 0.0, pltpu.roll(acc[2], cells - 1, 0))
    return acc[1] + left + right


def split(refs, *sizes):
    ends = np.cumsum((0,) + sizes)
    return [refs[a:b] for a, b in zip(ends[:-1], ends[1:])]


def first_kernel(info, stats, gain, shift, *refs):
    values, above, below, (held, first_ref, out, sem) = split(refs, TEAM, TEAM, TEAM, 4)
    zeros = jnp.zeros((WIDTH, CH), BF)
    for j, frame in enumerate(values):
        mean, scale = norm_table(join_stats(stats[:, 128 * j : 128 * j + 128]))
        table = (mean, scale * gain[0:1, :], shift[0:1, :])
        for row in range(ROWS):
            out[j, 1 + row] = norm(frame[row], table)
            if j == 0:
                first_ref[row] = out[0, 1 + row]
        out[j, 0] = jnp.where(info[1] == 1, zeros, norm(above[j][...], table))
        out[j, ROWS + 1] = jnp.where(info[2] == 1, zeros, norm(below[j][...], table))
    copy = pltpu.make_async_copy(out, held.at[0], sem)
    copy.start()
    copy.wait()


def conv_one_kernel(info, gain, shift, *refs):
    (stats,), inputs, earlier, (kernels,), outs, scratch = split(refs, 1, 1, TEAM, 1, 4, 4)
    hidden_ref, last_ref, top_ref, stats_ref = outs
    frames, weights, acc, sems = scratch
    parts = [stats[:, 128 * j : 128 * j + 128] for j in range(TEAM)]
    copies = start_loads(0, kernels, [inputs[0].at[0]], earlier, [frames.at[2]], weights, frames, sems)
    total = convolve(parts, copies, frames, weights, sems, acc).astype(BF)
    hidden_ref[...] = total.reshape(TEAM, ROWS, WIDTH, PART)
    for j in range(TEAM):
        last_ref[j] = hidden_ref[j, ROWS - 1]
        top_ref[j] = hidden_ref[j, 0]
    total = total.astype(F32)
    total = jnp.concatenate([total[j * CELLS : (j + 1) * CELLS] for j in range(TEAM)], axis=1)
    stats_ref[...] = flagged(local_stats(total), info[3])


def conv_two_kernel(info, gain, shift, *refs):
    (stats,), inputs, residual, earlier, (kernels,), outs, raw, scratch = split(
        refs, 1, TEAM, TEAM, TEAM, 1, TEAM + 1, 2 * TEAM, 4
    )
    frames, weights, acc, sems = scratch
    copies = start_loads(1, kernels, inputs + residual, earlier, raw, weights, frames, sems)
    parts = [stats[:, 128 * j : 128 * j + 128] for j in range(TEAM)]
    values, residual = split(raw, TEAM, TEAM)
    zeros = jnp.zeros((WIDTH, PART), BF)
    for k, (hidden, part) in enumerate(zip(values, parts)):
        mean, scale = norm_table(join_stats(part))
        lanes = pl.ds(pl.multiple_of((info[0] ^ k) * PART, PART), PART)
        gains, shifts = gain[1:2, lanes], shift[1:2, lanes]
        for j in range(TEAM):
            here = slice((j ^ k) * PART, (j ^ k) * PART + PART)
            table = (mean[:, here], scale[:, here] * gains, shifts)
            for row in range(ROWS + 2):
                values_row = norm(hidden[j ^ k, row], table)
                if row == 0:
                    values_row = jnp.where(info[1] == 1, zeros, values_row)
                elif row == ROWS + 1:
                    values_row = jnp.where(info[2] == 1, zeros, values_row)
                frames[2, j, row, :, lanes] = values_row
    for row in range(ROWS):
        outs[TEAM][row] = frames[2, 0, 1 + row]
    branch = convolve(parts, copies, frames, weights, sems, acc).reshape(TEAM, ROWS, WIDTH, PART)
    lanes = pl.ds(pl.multiple_of(info[0] * PART, PART), PART)
    for j in range(TEAM):
        for row in range(ROWS):
            joined = residual[j][row, :, lanes].astype(F32) + branch[j, row]
            outs[j][row] = joined.astype(BF)


def upsample_kernel(info, *refs):
    parts, out = refs[:-1], refs[-1]
    wide = lax.broadcasted_iota(jnp.int32, (2 * WIDTH, WIDTH), 0) // 2
    column = lax.broadcasted_iota(jnp.int32, (2 * WIDTH, WIDTH), 1)
    twice = jnp.where(wide == column, 1.0, 0.0).astype(BF)
    for j, part in enumerate(parts):
        lanes = pl.ds(pl.multiple_of((info[0] ^ j) * PART, PART), PART)
        values = jnp.dot(twice, part[0], preferred_element_type=F32).astype(BF)
        out[0, :, lanes] = values
        out[1, :, lanes] = values


def conv_call(kernel, name, out_shape, info, scales, stats, inputs, earlier, kernels, raw):
    return pl.pallas_call(
        kernel,
        out_shape=out_shape,
        in_specs=[SMEM] + [VMEM] * 3 + [HBM] * (len(inputs) + TEAM + 1),
        out_specs=tuple(VMEM for _ in out_shape),
        scratch_shapes=[pltpu.VMEM(array.shape, BF) for array in inputs[:raw]]
        + [
            pltpu.VMEM((3, TEAM, ROWS + 2, WIDTH, CH), BF),
            pltpu.VMEM((27, CH, PART), BF),
            pltpu.VMEM((3, TEAM * CELLS, PART), F32),
            pltpu.SemaphoreType.DMA((9 + len(inputs) + TEAM,)),
        ],
        compiler_params=pltpu.CompilerParams(vmem_limit_bytes=50 * 2**20),
        cost_estimate=pl.CostEstimate(
            flops=2 * 512 * 27 * CH * PART, bytes_accessed=12 * 10**6, transcendentals=10**6
        ),
        name=name,
    )(info, *scales, stats, *inputs, *earlier, kernels)


def per_device(
    generator_latents,
    column_holder_map,
    prior_frame_index,
    caches,
    kernel_weight_pair,
    group_norm_gain,
    group_norm_shift,
):
    tile = lax.axis_index("tile")
    part = lax.axis_index("req") % TEAM
    team = range(1, TEAM)

    shard = lax.dynamic_slice_in_dim(kernel_weight_pair, part * PART, PART, axis=3)
    kernels = lax.all_gather(shard, "tile", axis=2, tiled=True)

    placed = lax.all_to_all(generator_latents, "req", split_axis=0, concat_axis=0, tiled=True)

    position = prior_frame_index[0]
    info = jnp.stack([part, tile == 0, tile == TILES - 1, position == 0]).astype(jnp.int32)

    def history(rows):
        return jnp.stack([jnp.where(position >= 2, rows[:, 0], rows[:, 1]), rows[:, 1]], axis=1)

    above = beside(history(caches[0, :, :, ROWS - 1]), -1)
    below = beside(history(caches[0, :, :, 0]), 1)
    placed, above, below, earlier = lax.optimization_barrier((placed, above, below, caches[0]))
    earlier = history(earlier)


    def of_team(own):
        return [own] + [from_team(own, j) for j in team]

    old = [
        jnp.concatenate([above[conv][:, None], earlier[conv], below[conv][:, None]], axis=1)
        for conv in range(2)
    ]
    placed, old = lax.optimization_barrier((placed, old))
    old_one = of_team(old[0])

    owner = column_holder_map[0, :, 0]
    hits = (owner[:, None] == jnp.arange(TILES, dtype=jnp.int32)[None, :]).astype(jnp.int32)
    slot = jnp.sum((jnp.cumsum(hits, axis=0) - hits) * hits, axis=1)
    index = (owner * 16 + slot).astype(jnp.int32)[:, None]

    placed = lax.all_to_all(
        placed.reshape(TILES, 16, CH), "tile", split_axis=0, concat_axis=0, tiled=True
    )
    stats_shape = jax.ShapeDtypeStruct((TILES, 128), F32)
    frame, last, top, stats = pl.pallas_call(
        frame_kernel,
        out_shape=(shape(ROWS, WIDTH, CH), shape(WIDTH, CH), shape(WIDTH, CH), stats_shape),
        in_specs=[SMEM, VMEM, VMEM],
        out_specs=(VMEM, VMEM, VMEM, VMEM),
        compiler_params=pltpu.CompilerParams(vmem_limit_bytes=16 * 2**20),
        cost_estimate=pl.CostEstimate(flops=3 * 10**8, bytes_accessed=10**6, transcendentals=0),
        name="frame",
    )(info, index, placed)

    def exchange(values, last, top, stats):
        slots = [values] + [from_team(values, j) for j in team]
        above = [beside(last, -1, j) for j in range(TEAM)]
        below = [beside(top, 1, j) for j in range(TEAM)]
        stats = jnp.concatenate([stats] + [from_team(stats, j) for j in team], axis=1)
        stats = lax.all_to_all(stats, "tile", split_axis=0, concat_axis=0, tiled=True)
        return slots, stats, [*slots, *above, *below]

    scales = (group_norm_gain, group_norm_shift)
    frames, stats, inputs = exchange(frame, last, top, stats)
    inputs, late = lax.optimization_barrier((inputs, old[1]))
    old_two = of_team(late)
    current, first = pl.pallas_call(
        first_kernel,
        out_shape=(shape(HELD, TEAM, ROWS + 2, WIDTH, CH), shape(ROWS, WIDTH, CH)),
        in_specs=[SMEM] + [VMEM] * (3 + len(inputs)),
        out_specs=(HBM, VMEM),
        scratch_shapes=[pltpu.VMEM((TEAM, ROWS + 2, WIDTH, CH), BF), pltpu.SemaphoreType.DMA],
        compiler_params=pltpu.CompilerParams(vmem_limit_bytes=16 * 2**20),
        cost_estimate=pl.CostEstimate(
            flops=10**7, bytes_accessed=3 * 10**6, transcendentals=10**6
        ),
        name="first",
    )(info, stats, *scales, *inputs)
    hidden, last, top, stats = conv_call(
        conv_one_kernel,
        "conv_one",
        (shape(TEAM, ROWS, WIDTH, PART),)
        + (shape(TEAM, WIDTH, PART),) * 2
        + (stats_shape,),
        info,
        scales,
        stats,
        [current],
        old_one,
        kernels,
        0,
    )
    above, below = beside(last, -1), beside(top, 1)
    stats = jnp.concatenate([stats] + [from_team(stats, j) for j in team], axis=1)
    above, below, stats = lax.optimization_barrier((above, below, stats))
    current = jnp.concatenate([above[:, None], hidden, below[:, None]], axis=1)
    inputs = [current] + [from_team(current, j) for j in team]
    stats = lax.all_to_all(stats, "tile", split_axis=0, concat_axis=0, tiled=True)
    *joined, second = conv_call(
        conv_two_kernel,
        "conv_two",
        (shape(ROWS, WIDTH, PART),) * TEAM + (shape(ROWS, WIDTH, CH),),
        info,
        scales,
        stats,
        inputs + frames,
        old_two,
        kernels,
        2 * TEAM,
    )
    joined = [joined[0]] + [from_team(joined[j], j) for j in team]
    upsampled = pl.pallas_call(
        upsample_kernel,
        out_shape=shape(2 * ROWS, 2 * WIDTH, CH),
        grid=(ROWS,),
        in_specs=[SMEM] + [pl.BlockSpec((1, WIDTH, PART), lambda i: (i, 0, 0))] * TEAM,
        out_specs=pl.BlockSpec((2, 2 * WIDTH, CH), lambda i: (i, 0, 0)),
        compiler_params=pltpu.CompilerParams(vmem_limit_bytes=16 * 2**20),
        cost_estimate=pl.CostEstimate(flops=10**8, bytes_accessed=2 * 10**6, transcendentals=0),
        name="upsample",
    )(info, *joined)
    return (upsampled[None], jnp.stack([first, second])[None])


def solution(mesh):
    in_specs = (
        P(None, "req", "tile", None, None),
        P("req", None, None),
        P("req"),
        P("req", None, None, "tile", None, None),
        P(None, None, "tile", None),
        P(),
        P(),
    )
    out_specs = (P("req", "tile", None, None), P("req", None, "tile", None, None))
    return jax.shard_map(
        per_device, mesh=mesh, in_specs=in_specs, out_specs=out_specs, check_vma=False
    )
```

```python
import functools

import jax
import jax.numpy as jnp
import numpy as np
from jax import lax
from jax.experimental import pallas as pl
from jax.experimental.pallas import tpu as pltpu
from jax.sharding import PartitionSpec as P

GROUPS = 32
EPS = 1e-06
CH = 512
TEAM = 2
PART = CH // TEAM
PER = CH // GROUPS
WIDTH = 128
ROWS = 2
CELLS = ROWS * WIDTH
TILES = 32
HELD = 16
TAP_ORDER = (2, 0, 1)
BF, F32 = jnp.bfloat16, jnp.float32


def from_team(array, j):
    return lax.ppermute(array, "req", [(i, i ^ j) for i in range(8)])


def beside(array, step, j=0):
    perm = []
    for i in range(8):
        for t in range(TILES):
            if 0 <= t + step < TILES:
                perm.append(((i ^ j) * TILES + t + step, i * TILES + t))
    return lax.ppermute(array, ("req", "tile"), perm)


dot32 = functools.partial(jnp.dot, preferred_element_type=F32, precision=lax.Precision.HIGHEST)


def spread_lanes(channels, first_lane, transposed=False):
    shape = (128, channels) if transposed else (channels, 128)
    lane = lax.broadcasted_iota(jnp.int32, shape, 0 if transposed else 1)
    channel = lax.broadcasted_iota(jnp.int32, shape, 1 if transposed else 0)
    return jnp.where(lane == first_lane + channel // PER, 1.0, 0.0).astype(F32)


def local_stats(values):
    cells, channels = values.shape
    total = jnp.sum(values, axis=0, keepdims=True) / (cells * PER)
    mean = dot32(jnp.broadcast_to(total, (8, channels)), spread_lanes(channels, 0))
    off = values - dot32(mean, spread_lanes(channels, 0, True))[:1]
    square = jnp.broadcast_to(jnp.sum(off * off, axis=0, keepdims=True), (8, channels))
    return mean + dot32(square, spread_lanes(channels, GROUPS))


def join_stats(stats):
    lane = lax.broadcasted_iota(jnp.int32, (TILES, 128), 1)
    mean = jnp.sum(jnp.where(lane < GROUPS, stats, 0.0), axis=0, keepdims=True) / TILES
    off = jnp.where(lane < GROUPS, stats - mean, 0.0)
    between = jnp.sum(off * off, axis=0, keepdims=True) / TILES
    within = jnp.where(lane >= GROUPS, stats, 0.0)
    within = jnp.sum(within, axis=0, keepdims=True) / (TILES * CELLS * PER)
    return tuple(jnp.broadcast_to(v, (8, 128)) for v in (mean, within, between))


def norm_table(joined):
    mean, within, between = joined
    back = spread_lanes(CH, 0, True)
    spread = dot32(within, spread_lanes(CH, GROUPS, True)) + dot32(between, back)
    return dot32(mean, back)[:1], lax.rsqrt(spread[:1] + EPS)


def flagged(stats, flag):
    lane = lax.broadcasted_iota(jnp.int32, (TILES, 128), 1)
    return jnp.where(lane == 64, flag.astype(F32), jnp.broadcast_to(stats[:1], (TILES, 128)))


def flag_of(stats):
    lane = lax.broadcasted_iota(jnp.int32, (8, 128), 1)
    return jnp.max(jnp.where(lane == 64, stats[0:8, :], 0.0)) > 0.5


def silu(v):
    return v / (1.0 + jnp.exp(-v))


def norm(values, table):
    return silu((values.astype(F32) - table[0]) * table[1] + table[2]).astype(BF)


def frame_kernel(info, index_ref, placed_ref, frame_ref, last_ref, first_ref, stats_ref):
    index = index_ref[...]
    lane = lax.broadcasted_iota(jnp.int32, (WIDTH, CH), 1)
    placed = placed_ref[...].reshape(CH, CH)
    rows = []
    for row in range(ROWS):
        pick = jnp.where(lane == index + 8 * row, 1.0, 0.0).astype(BF)
        rows.append(jnp.dot(pick, placed, preferred_element_type=F32))
        frame_ref[row] = rows[row].astype(BF)
    last_ref[...] = frame_ref[ROWS - 1]
    first_ref[...] = frame_ref[0]
    stats_ref[...] = flagged(local_stats(jnp.concatenate(rows, axis=0)), info[3])


VMEM = pl.BlockSpec(memory_space=pltpu.VMEM)
SMEM = pl.BlockSpec(memory_space=pltpu.SMEM)
HBM = pl.BlockSpec(memory_space=pltpu.HBM)


def shape(*sizes):
    return jax.ShapeDtypeStruct(sizes, BF)


def start_loads(conv, kernels, inputs, earlier, raw, weights, frames, sems):
    pairs = list(zip(inputs, raw)) + [(earlier[j], frames.at[pl.ds(0, 2), j]) for j in range(TEAM)]
    copies = [pltpu.make_async_copy(src, dst, sems.at[9 + k]) for k, (src, dst) in enumerate(pairs)]
    first, later = copies[: len(inputs)], copies[len(inputs) :]
    for copy in first:
        copy.start()
    for a in TAP_ORDER:
        for b in range(3):
            part = pl.ds(9 * a + 3 * b, 3)
            sem = sems.at[3 * a + b]
            pltpu.make_async_copy(kernels.at[conv, part], weights.at[part], sem).start()
        for copy in later if a == 2 else ():
            copy.start()
    for copy in first:
        copy.wait()
    return later


def finish_history(parts, copies, frames):
    for copy in copies:
        copy.wait()
    for j, part in enumerate(parts):

        @pl.when(flag_of(part))
        def _():
            for row in range(ROWS + 2):
                frames[0, j, row] = frames[2, j, row]
                frames[1, j, row] = frames[2, j, row]


def convolve(parts, copies, frames, weights, sems, acc):
    cells = TEAM * CELLS
    for a in TAP_ORDER:
        if a == 0:
            finish_history(parts, copies, frames)
        for b in range(3):
            part = weights.at[pl.ds(9 * a + 3 * b, 3)]
            pltpu.make_async_copy(part, part, sems.at[3 * a + b]).wait()
        for j in range(TEAM):
            here = pl.ds(j * CELLS, CELLS)
            for c in range(3):
                total = None if a == 2 else acc[c, here]
                for b in range(3):
                    slab = frames[a, j, pl.ds(b, ROWS)].reshape(CELLS, CH)
                    tap = weights[9 * a + 3 * b + c]
                    product = jnp.dot(slab, tap, preferred_element_type=F32)
                    total = product if total is None else total + product
                acc[c, here] = total
    column = lax.broadcasted_iota(jnp.int32, (cells, PART), 0) % WIDTH
    left = jnp.where(column == 0, 0.0, pltpu.roll(acc[0], 1, 0))
    right = jnp.where(column == WIDTH - 1, 0.0, pltpu.roll(acc[2], cells - 1, 0))
    return acc[1] + left + right


def split(refs, *sizes):
    ends = np.cumsum((0,) + sizes)
    return [refs[a:b] for a, b in zip(ends[:-1], ends[1:])]


def first_kernel(info, stats, gain, shift, *refs):
    values, above, below, (held, first_ref, out, sem) = split(refs, TEAM, TEAM, TEAM, 4)
    zeros = jnp.zeros((WIDTH, CH), BF)
    for j, frame in enumerate(values):
        mean, scale = norm_table(join_stats(stats[:, 128 * j : 128 * j + 128]))
        table = (mean, scale * gain[0:1, :], shift[0:1, :])
        for row in range(ROWS):
            out[j, 1 + row] = norm(frame[row], table)
            if j == 0:
                first_ref[row] = out[0, 1 + row]
        out[j, 0] = jnp.where(info[1] == 1, zeros, norm(above[j][...], table))
        out[j, ROWS + 1] = jnp.where(info[2] == 1, zeros, norm(below[j][...], table))
    copy = pltpu.make_async_copy(out, held.at[0], sem)
    copy.start()
    copy.wait()


def conv_one_kernel(info, gain, shift, *refs):
    (stats,), inputs, earlier, (kernels,), outs, scratch = split(refs, 1, 1, TEAM, 1, 4, 4)
    hidden_ref, last_ref, top_ref, stats_ref = outs
    frames, weights, acc, sems = scratch
    parts = [stats[:, 128 * j : 128 * j + 128] for j in range(TEAM)]
    copies = start_loads(0, kernels, [inputs[0].at[0]], earlier, [frames.at[2]], weights, frames, sems)
    total = convolve(parts, copies, frames, weights, sems, acc).astype(BF)
    hidden_ref[...] = total.reshape(TEAM, ROWS, WIDTH, PART)
    for j in range(TEAM):
        last_ref[j] = hidden_ref[j, ROWS - 1]
        top_ref[j] = hidden_ref[j, 0]
    total = total.astype(F32)
    total = jnp.concatenate([total[j * CELLS : (j + 1) * CELLS] for j in range(TEAM)], axis=1)
    stats_ref[...] = flagged(local_stats(total), info[3])


def conv_two_kernel(info, gain, shift, *refs):
    (stats,), inputs, residual, earlier, (kernels,), outs, raw, scratch = split(
        refs, 1, TEAM, TEAM, TEAM, 1, TEAM + 1, 2 * TEAM, 4
    )
    frames, weights, acc, sems = scratch
    copies = start_loads(1, kernels, inputs + residual, earlier, raw, weights, frames, sems)
    parts = [stats[:, 128 * j : 128 * j + 128] for j in range(TEAM)]
    values, residual = split(raw, TEAM, TEAM)
    zeros = jnp.zeros((WIDTH, PART), BF)
    for k, (hidden, part) in enumerate(zip(values, parts)):
        mean, scale = norm_table(join_stats(part))
        lanes = pl.ds(pl.multiple_of((info[0] ^ k) * PART, PART), PART)
        gains, shifts = gain[1:2, lanes], shift[1:2, lanes]
        for j in range(TEAM):
            here = slice((j ^ k) * PART, (j ^ k) * PART + PART)
            table = (mean[:, here], scale[:, here] * gains, shifts)
            for row in range(ROWS + 2):
                values_row = norm(hidden[j ^ k, row], table)
                if row == 0:
                    values_row = jnp.where(info[1] == 1, zeros, values_row)
                elif row == ROWS + 1:
                    values_row = jnp.where(info[2] == 1, zeros, values_row)
                frames[2, j, row, :, lanes] = values_row
    for row in range(ROWS):
        outs[TEAM][row] = frames[2, 0, 1 + row]
    branch = convolve(parts, copies, frames, weights, sems, acc).reshape(TEAM, ROWS, WIDTH, PART)
    lanes = pl.ds(pl.multiple_of(info[0] * PART, PART), PART)
    for j in range(TEAM):
        for row in range(ROWS):
            joined = residual[j][row, :, lanes].astype(F32) + branch[j, row]
            outs[j][row] = joined.astype(BF)


def upsample_kernel(info, *refs):
    parts, out = refs[:-1], refs[-1]
    wide = lax.broadcasted_iota(jnp.int32, (2 * WIDTH, WIDTH), 0) // 2
    column = lax.broadcasted_iota(jnp.int32, (2 * WIDTH, WIDTH), 1)
    twice = jnp.where(wide == column, 1.0, 0.0).astype(BF)
    for j, part in enumerate(parts):
        lanes = pl.ds(pl.multiple_of((info[0] ^ j) * PART, PART), PART)
        values = jnp.dot(twice, part[0], preferred_element_type=F32).astype(BF)
        out[0, :, lanes] = values
        out[1, :, lanes] = values


def conv_call(kernel, name, out_shape, info, scales, stats, inputs, earlier, kernels, raw):
    return pl.pallas_call(
        kernel,
        out_shape=out_shape,
        in_specs=[SMEM] + [VMEM] * 3 + [HBM] * (len(inputs) + TEAM + 1),
        out_specs=tuple(VMEM for _ in out_shape),
        scratch_shapes=[pltpu.VMEM(array.shape, BF) for array in inputs[:raw]]
        + [
            pltpu.VMEM((3, TEAM, ROWS + 2, WIDTH, CH), BF),
            pltpu.VMEM((27, CH, PART), BF),
            pltpu.VMEM((3, TEAM * CELLS, PART), F32),
            pltpu.SemaphoreType.DMA((9 + len(inputs) + TEAM,)),
        ],
        compiler_params=pltpu.CompilerParams(vmem_limit_bytes=50 * 2**20),
        cost_estimate=pl.CostEstimate(
            flops=2 * 512 * 27 * CH * PART, bytes_accessed=12 * 10**6, transcendentals=10**6
        ),
        name=name,
    )(info, *scales, stats, *inputs, *earlier, kernels)


def per_device(
    generator_latents,
    column_holder_map,
    prior_frame_index,
    caches,
    kernel_weight_pair,
    group_norm_gain,
    group_norm_shift,
):
    tile = lax.axis_index("tile")
    part = lax.axis_index("req") % TEAM
    team = range(1, TEAM)

    shard = lax.dynamic_slice_in_dim(kernel_weight_pair, part * PART, PART, axis=3)
    kernels = lax.all_gather(shard, "tile", axis=2, tiled=True)

    placed = lax.all_to_all(generator_latents, "req", split_axis=0, concat_axis=0, tiled=True)

    position = prior_frame_index[0]
    info = jnp.stack([part, tile == 0, tile == TILES - 1, position == 0]).astype(jnp.int32)

    def history(rows):
        return jnp.stack([jnp.where(position >= 2, rows[:, 0], rows[:, 1]), rows[:, 1]], axis=1)

    above = beside(history(caches[0, :, :, ROWS - 1]), -1)
    below = beside(history(caches[0, :, :, 0]), 1)
    placed, above, below, earlier = lax.optimization_barrier((placed, above, below, caches[0]))
    earlier = history(earlier)


    def of_team(own):
        return [own] + [from_team(own, j) for j in team]

    old = [
        jnp.concatenate([above[conv][:, None], earlier[conv], below[conv][:, None]], axis=1)
        for conv in range(2)
    ]
    placed, old[0] = lax.optimization_barrier((placed, old[0]))
    old_one = of_team(old[0])

    owner = column_holder_map[0, :, 0]
    hits = (owner[:, None] == jnp.arange(TILES, dtype=jnp.int32)[None, :]).astype(jnp.int32)
    slot = jnp.sum((jnp.cumsum(hits, axis=0) - hits) * hits, axis=1)
    index = (owner * 16 + slot).astype(jnp.int32)[:, None]

    placed = lax.all_to_all(
        placed.reshape(TILES, 16, CH), "tile", split_axis=0, concat_axis=0, tiled=True
    )
    stats_shape = jax.ShapeDtypeStruct((TILES, 128), F32)
    frame, last, top, stats = pl.pallas_call(
        frame_kernel,
        out_shape=(shape(ROWS, WIDTH, CH), shape(WIDTH, CH), shape(WIDTH, CH), stats_shape),
        in_specs=[SMEM, VMEM, VMEM],
        out_specs=(VMEM, VMEM, VMEM, VMEM),
        compiler_params=pltpu.CompilerParams(vmem_limit_bytes=16 * 2**20),
        cost_estimate=pl.CostEstimate(flops=3 * 10**8, bytes_accessed=10**6, transcendentals=0),
        name="frame",
    )(info, index, placed)

    def exchange(values, last, top, stats):
        slots = [values] + [from_team(values, j) for j in team]
        above = [beside(last, -1, j) for j in range(TEAM)]
        below = [beside(top, 1, j) for j in range(TEAM)]
        stats = jnp.concatenate([stats] + [from_team(stats, j) for j in team], axis=1)
        stats = lax.all_to_all(stats, "tile", split_axis=0, concat_axis=0, tiled=True)
        return slots, stats, [*slots, *above, *below]

    scales = (group_norm_gain, group_norm_shift)
    frames, stats, inputs = exchange(frame, last, top, stats)
    inputs, late = lax.optimization_barrier((inputs, old[1]))
    old_two = of_team(late)
    current, first = pl.pallas_call(
        first_kernel,
        out_shape=(shape(HELD, TEAM, ROWS + 2, WIDTH, CH), shape(ROWS, WIDTH, CH)),
        in_specs=[SMEM] + [VMEM] * (3 + len(inputs)),
        out_specs=(HBM, VMEM),
        scratch_shapes=[pltpu.VMEM((TEAM, ROWS + 2, WIDTH, CH), BF), pltpu.SemaphoreType.DMA],
        compiler_params=pltpu.CompilerParams(vmem_limit_bytes=16 * 2**20),
        cost_estimate=pl.CostEstimate(
            flops=10**7, bytes_accessed=3 * 10**6, transcendentals=10**6
        ),
        name="first",
    )(info, stats, *scales, *inputs)
    hidden, last, top, stats = conv_call(
        conv_one_kernel,
        "conv_one",
        (shape(TEAM, ROWS, WIDTH, PART),)
        + (shape(TEAM, WIDTH, PART),) * 2
        + (stats_shape,),
        info,
        scales,
        stats,
        [current],
        old_one,
        kernels,
        0,
    )
    above, below = beside(last, -1), beside(top, 1)
    stats = jnp.concatenate([stats] + [from_team(stats, j) for j in team], axis=1)
    above, below, stats = lax.optimization_barrier((above, below, stats))
    current = jnp.concatenate([above[:, None], hidden, below[:, None]], axis=1)
    inputs = [current] + [from_team(current, j) for j in team]
    stats = lax.all_to_all(stats, "tile", split_axis=0, concat_axis=0, tiled=True)
    *joined, second = conv_call(
        conv_two_kernel,
        "conv_two",
        (shape(ROWS, WIDTH, PART),) * TEAM + (shape(ROWS, WIDTH, CH),),
        info,
        scales,
        stats,
        inputs + frames,
        old_two,
        kernels,
        2 * TEAM,
    )
    joined = [joined[0]] + [from_team(joined[j], j) for j in team]
    upsampled = pl.pallas_call(
        upsample_kernel,
        out_shape=shape(2 * ROWS, 2 * WIDTH, CH),
        grid=(ROWS,),
        in_specs=[SMEM] + [pl.BlockSpec((1, WIDTH, PART), lambda i: (i, 0, 0))] * TEAM,
        out_specs=pl.BlockSpec((2, 2 * WIDTH, CH), lambda i: (i, 0, 0)),
        compiler_params=pltpu.CompilerParams(vmem_limit_bytes=16 * 2**20),
        cost_estimate=pl.CostEstimate(flops=10**8, bytes_accessed=2 * 10**6, transcendentals=0),
        name="upsample",
    )(info, *joined)
    return (upsampled[None], jnp.stack([first, second])[None])


def solution(mesh):
    in_specs = (
        P(None, "req", "tile", None, None),
        P("req", None, None),
        P("req"),
        P("req", None, None, "tile", None, None),
        P(None, None, "tile", None),
        P(),
        P(),
    )
    out_specs = (P("req", "tile", None, None), P("req", None, "tile", None, None))
    return jax.shard_map(
        per_device, mesh=mesh, in_specs=in_specs, out_specs=out_specs, check_vma=False
    )
```
